32 devices in a mesh: grp: 2 (over x), seq: 16 (over z, y, core).
Axes of the slice: x: 2, y: 2, z: 4, core: 2. Of those that a mesh axis runs over, the one named last changes fastest.
Arguments:
- queries: bfloat16 [4096, 3072], P(('grp', 'seq')), parts along dimension 0, may hold values from -6 to 6
- keys: bfloat16 [4096, 3072], P(('grp', 'seq')), parts along dimension 0, may hold values from -6 to 6
- values: bfloat16 [4096, 3072], P(('grp', 'seq')), parts along dimension 0, may hold values from -6 to 6
- text_keys: bfloat16 [512, 3072], P('grp'), parts along dimension 0, may hold values from -6 to 6
- text_values: bfloat16 [512, 3072], P('grp'), parts along dimension 0, may hold values from -6 to 6
- text_len: int32 [2], P('grp'), parts along dimension 0, may hold values from 64 to 256
- plan: int32 [12], P('grp'), parts along dimension 0, may hold values from 0 to 9
- deltas: bfloat16 [6, 4096, 3072], P(None, ('grp', 'seq')), parts along dimension 1, may hold values from -2 to 2
Outputs:
- mixed: bfloat16 [4096, 3072], P(('grp', 'seq')), parts along dimension 0
The draws below stay inside these ranges and needn't reach their ends.
There are 2 independent parts, one for each index of `grp`. The reference program is written for one: setup_inputs(seed, part) draws one part's arguments, and reference() takes and returns one part's arrays. A program takes and returns all parts, laid end to end along the dimension named above; each array names one. Nothing has to cross between parts.
All inputs are finite; a program needn't handle non-finite values.
Results may differ from the reference program's by a relative error of at most 0.0034.
Values may be sent and summed in bfloat16 or wider, within the bound.
No kernel may reach another device: no remote copies, remote signals or barrier semaphores. Data moves between devices by JAX's collectives and lax.ppermute only.
A program may use at most 128 MiB of HBM per device.

```python
import jax
import jax.numpy as jnp
from jax import lax

HEADS = 24
HEAD_DIM = 128
TEXT = 256
BLOCKS = 6
VIDEO_TOKENS = 2048


def draw_queries(key, part):
    key = jax.random.fold_in(key, 11)
    shape = (VIDEO_TOKENS, HEADS * HEAD_DIM)
    result = 1.6 * jax.random.truncated_normal(key, -3.7, 3.7, shape, jnp.float32)
    return result.astype(jnp.bfloat16)


def draw_keys(key, part):
    key = jax.random.fold_in(key, 23)
    shape = (VIDEO_TOKENS, HEADS * HEAD_DIM)
    result = 1.6 * jax.random.truncated_normal(key, -3.7, 3.7, shape, jnp.float32)
    return result.astype(jnp.bfloat16)


def with_ends(values, rng, least, largest):
    spot = [jax.random.randint(jax.random.fold_in(rng, axis), (), 0, length) for axis, length in enumerate(values.shape)]
    widest = values.shape.index(max(values.shape))
    neighbour = spot[:widest] + [(spot[widest] + 1) % values.shape[widest]] + spot[widest + 1:]
    return values.at[tuple(spot)].set(least).at[tuple(neighbour)].set(largest)


def levels(key, shape, split, smallest, top_value):
    gain, own = 1.0, jax.random.fold_in(key, 6)
    for dim, blocks in split:
        heights = jnp.exp(jax.random.uniform(jax.random.fold_in(own, dim), (blocks,), jnp.float32, smallest / len(split), top_value / len(split)))
        gain = gain * jnp.repeat(heights, shape[dim] // blocks).reshape([-1 if axis == dim else 1 for axis in range(len(shape))])
    return gain


def centred(rng, shape, spread, most, cuts=(), held_as=jnp.bfloat16):
    loudness = levels(rng, shape, cuts, -0.22, 0.18) if cuts else 1.0
    entries = jax.random.normal(rng, shape, jnp.float32) * spread * loudness
    return jnp.minimum(jnp.maximum(entries, -most), most).astype(held_as)


def setup_inputs(seed: int = 0, part: int = 0) -> dict:
    streams_of = jax.random.split(jax.random.key(seed), 9)
    own_keys = jax.random.split(jax.random.fold_in(streams_of[8], part), 9)
    return {
        "queries": draw_queries(jax.random.fold_in(jax.random.fold_in(streams_of[8], part), 71), part),
        "keys": draw_keys(jax.random.fold_in(jax.random.fold_in(streams_of[8], part), 71), part),
        "values": centred(own_keys[2], (VIDEO_TOKENS, HEADS * HEAD_DIM), 1.0, 6.0, ((0, 16),)),
        "text_keys": centred(own_keys[3], (TEXT, HEADS * HEAD_DIM), 1.6, 6.0),
        "text_values": centred(own_keys[4], (TEXT, HEADS * HEAD_DIM), 1.0, 6.0),
        "text_len": jax.random.randint(own_keys[5], (1,), TEXT // 4, TEXT + 1).astype(jnp.int32),
        "plan": with_ends(jax.random.randint(own_keys[6], (BLOCKS,), 0, 10), jax.random.fold_in(own_keys[6], 1), 0, 9).astype(jnp.int32),
        "deltas": centred(own_keys[7], (BLOCKS, VIDEO_TOKENS, HEADS * HEAD_DIM), 0.3, 2.0, ((1, 16),)),
    }


def heads_first(array):
    return array.reshape(array.shape[0], HEADS, HEAD_DIM).transpose(1, 0, 2)


def reference(queries, keys, values, text_keys, text_values, text_len, plan, deltas):
    score_scale = HEAD_DIM ** -0.5
    usable = jnp.arange(TEXT) < text_len[0]

    def one_head(operands):
        head_q, head_k, head_v, head_tk, head_tv = operands
        video_scores = jnp.dot(head_q, head_k.T, preferred_element_type=jnp.float32) * score_scale
        text_scores = jnp.dot(head_q, head_tk.T, preferred_element_type=jnp.float32) * score_scale
        text_scores = jnp.where(usable[None, :], text_scores, -jnp.inf)
        row_top = jnp.maximum(jnp.max(video_scores, axis=1), jnp.max(text_scores, axis=1))[:, None]
        video_exp = jnp.exp(video_scores - row_top)
        text_exp = jnp.exp(text_scores - row_top)
        denominator = jnp.sum(video_exp, axis=1) + jnp.sum(text_exp, axis=1)
        weighted = jnp.dot(video_exp.astype(jnp.bfloat16), head_v, preferred_element_type=jnp.float32)
        weighted = weighted + jnp.dot(text_exp.astype(jnp.bfloat16), head_tv, preferred_element_type=jnp.float32)
        return weighted / denominator[:, None]

    context = lax.map(one_head, (heads_first(queries), heads_first(keys), heads_first(values),
                                 heads_first(text_keys), heads_first(text_values)))
    context = context.transpose(1, 0, 2).reshape(VIDEO_TOKENS, HEADS * HEAD_DIM).astype(jnp.bfloat16)
    added = jnp.einsum('b,btc->tc', plan.astype(jnp.float32), deltas.astype(jnp.float32)) * 0.25
    return (context.astype(jnp.float32) + added).astype(jnp.bfloat16)
```

```python
import functools
import math

import jax
import jax.numpy as jnp
from jax import lax
from jax.experimental import pallas as pl
from jax.experimental.pallas import tpu as pltpu
from jax.sharding import PartitionSpec as P

HEADS = 24
HEAD_DIM = 128
HEADS_DEV = 3
PLANE = 4
PAIR = 2 * HEAD_DIM
EXP_SCALE = HEAD_DIM ** (-0.5) * math.log2(math.e)


def pack_kernel(spans, planes, where, *refs):
    n_src = 1 + max(source for source, _ in spans)
    sources, outs, sems = refs[:n_src], refs[n_src:-1], refs[-1]
    copies = []
    for relative in range(planes):
        plane = jnp.bitwise_xor(where[0], relative)
        for slot, (source, base) in enumerate(spans):
            start = pl.multiple_of(base + plane * PAIR, PAIR)
            copies.append(
                pltpu.make_async_copy(
                    sources[source].at[:, pl.ds(start, PAIR)],
                    outs[relative].at[:, pl.ds(slot * PAIR, PAIR)],
                    sems.at[relative, slot],
                )
            )
    for copy in copies:
        copy.start()
    for copy in copies:
        copy.wait()


def pack(where, spans, planes, *sources):
    rows = sources[0].shape[0]
    shape = jax.ShapeDtypeStruct((rows, len(spans) * PAIR), sources[0].dtype)
    return pl.pallas_call(
        functools.partial(pack_kernel, spans, planes),
        out_shape=[shape] * planes,
        in_specs=[pl.BlockSpec(memory_space=pltpu.SMEM)] + [pl.BlockSpec(memory_space=pl.ANY)] * len(sources),
        out_specs=[pl.BlockSpec(memory_space=pl.ANY)] * planes,
        scratch_shapes=[pltpu.SemaphoreType.DMA((planes, len(spans)))],
        name="pack",
    )(where, *sources)


def attend_kernel(n_q, n_kv, scalars, *refs):
    queries = refs[:n_q]
    keys = refs[n_q : n_q + n_kv]
    values = refs[n_q + n_kv : n_q + 2 * n_kv]
    text_keys, text_values = refs[n_q + 2 * n_kv : n_q + 2 * n_kv + 2]
    outs = refs[n_q + 2 * n_kv + 2 :]
    text_slots = text_keys.shape[0]
    contract_last = (((1,), (1,)), ((), ()))
    for first in range(0, n_q, 2):
        q = jnp.concatenate([queries[first][...], queries[first + 1][...]], axis=0)
        rows = q.shape[0]
        scores = [
            lax.dot_general(q, k[...], contract_last, preferred_element_type=jnp.float32) for k in keys
        ]
        text_scores = lax.dot_general(q, text_keys[...], contract_last, preferred_element_type=jnp.float32)
        usable = lax.broadcasted_iota(jnp.int32, (rows, text_slots), 1) < scalars[1]
        scores.append(jnp.where(usable, text_scores, -jnp.inf))
        top = functools.reduce(jnp.maximum, [jnp.max(s, axis=1, keepdims=True) for s in scores])
        total = jnp.zeros((rows, 1), jnp.float32)
        weighted = jnp.zeros((rows, HEAD_DIM), jnp.float32)
        for s, v in zip(scores, (*values, text_values)):
            weights = jnp.exp2((s - top) * EXP_SCALE)
            total = total + jnp.sum(weights, axis=1, keepdims=True)
            weighted = weighted + jnp.dot(
                weights.astype(jnp.bfloat16), v[...], preferred_element_type=jnp.float32
            )
        context = (weighted / total).astype(jnp.bfloat16)
        half = rows // 2
        outs[first][...] = context[:half]
        outs[first + 1][...] = context[half:]


def attend_pair(scalars, queries, q_block, kvs, text_keys, text_values, text_block):
    n_q, n_kv = len(queries), len(kvs)
    rows = queries[0].shape[0]
    slots = text_keys.shape[0]

    def column(block):
        return lambda head, scalars: (0, block + head)

    def text_column(head, scalars):
        return (0, text_block + scalars[0] * 2 + head)

    in_specs = [pl.BlockSpec((rows, HEAD_DIM), column(q_block)) for _ in queries]
    in_specs += [pl.BlockSpec((kv.shape[0], HEAD_DIM), column(0)) for kv in kvs]
    in_specs += [pl.BlockSpec((kv.shape[0], HEAD_DIM), column(2)) for kv in kvs]
    in_specs += [pl.BlockSpec((slots, HEAD_DIM), text_column)] * 2
    n_keys = sum(kv.shape[0] for kv in kvs) + slots
    work = 2 * n_q * rows * n_keys
    return pl.pallas_call(
        functools.partial(attend_kernel, n_q, n_kv),
        grid_spec=pltpu.PrefetchScalarGridSpec(
            num_scalar_prefetch=1,
            grid=(2,),
            in_specs=in_specs,
            out_specs=[pl.BlockSpec((rows, HEAD_DIM), column(0)) for _ in queries],
        ),
        out_shape=[jax.ShapeDtypeStruct((rows, PAIR), jnp.bfloat16)] * n_q,
        compiler_params=pltpu.CompilerParams(vmem_limit_bytes=40 * 1024 * 1024),
        cost_estimate=pl.CostEstimate(
            flops=work * HEAD_DIM * 4, bytes_accessed=4 * n_keys * PAIR, transcendentals=work
        ),
        name="attend",
    )(scalars, *queries, *kvs, *kvs, text_keys, text_values)


def deltas_kernel(plan, deltas, out):
    total = plan[0].astype(jnp.float32) * deltas[0].astype(jnp.float32)
    for block in range(1, deltas.shape[0]):
        total = total + plan[block].astype(jnp.float32) * deltas[block].astype(jnp.float32)
    out[...] = total * 0.25


def sum_deltas(plan, deltas):
    blocks, rows, width = deltas.shape
    step = width // 4
    return pl.pallas_call(
        deltas_kernel,
        grid=(4,),
        in_specs=[
            pl.BlockSpec(memory_space=pltpu.SMEM),
            pl.BlockSpec((blocks, rows, step), lambda i: (0, 0, i)),
        ],
        out_specs=pl.BlockSpec((rows, step), lambda i: (0, i)),
        out_shape=jax.ShapeDtypeStruct((rows, width), jnp.float32),
        cost_estimate=pl.CostEstimate(
            flops=2 * blocks * rows * width, bytes_accessed=2 * blocks * rows * width, transcendentals=0
        ),
        name="deltas",
    )(plan, deltas)


def mix_kernel(planes, where, added, *refs):
    pieces, out = refs[:-1], refs[-1]
    slab = planes * PAIR
    for index, piece in enumerate(pieces):
        phase, relative = divmod(index, planes)
        plane = jnp.bitwise_xor(where[0], relative)
        columns = pl.ds(pl.multiple_of(phase * slab + plane * PAIR, PAIR), PAIR)
        out[:, columns] = (piece[...].astype(jnp.float32) + added[:, columns]).astype(out.dtype)


def mix(where, planes, added, pieces):
    vmem = pl.BlockSpec(memory_space=pltpu.VMEM)
    return pl.pallas_call(
        functools.partial(mix_kernel, planes),
        in_specs=[pl.BlockSpec(memory_space=pltpu.SMEM)] + [vmem] * (1 + len(pieces)),
        out_specs=vmem,
        out_shape=jax.ShapeDtypeStruct(added.shape, jnp.bfloat16),
        name="mix",
    )(where, added, *pieces)


def plane_body(queries, keys, values, text_keys, text_values, text_len, plan, deltas):
    size = lax.axis_size("seq")
    planes = size // PLANE
    slab = planes * PAIR
    phases = HEADS * HEAD_DIM // slab
    plane = lax.axis_index("seq") // PLANE
    where = plane.astype(jnp.int32).reshape(1)
    scalars = jnp.concatenate([where, text_len])

    def swap(array, distance):
        return lax.ppermute(array, "seq", [(i, i ^ distance) for i in range(size)])

    def to_planes(pieces):
        return [pieces[0]] + [swap(pieces[r], PLANE * r) for r in range(1, planes)]

    def gather_plane(pieces):
        own = jnp.concatenate(pieces, axis=0)
        other = swap(own, 2)
        return [own, other, swap(own, 1), swap(other, 1)]

    first = to_planes(pack(where, ((0, 0), (1, 0), (2, 0)), planes, queries, keys, values))
    rest = [
        to_planes(pack(where, ((0, slab * p), (1, slab * p)), planes, keys, values)) for p in range(1, phases)
    ]
    later = to_planes(pack(where, tuple((0, slab * p) for p in range(1, phases)), planes, queries))

    gathered = [gather_plane([piece[:, PAIR:] for piece in first])] + [gather_plane(r) for r in rest]
    added = sum_deltas(plan, deltas)
    returned = []
    for p in range(phases):
        pieces, block = (first, 0) if p == 0 else (later, 2 * (p - 1))
        contexts = attend_pair(
            scalars, pieces, block, gathered[p], text_keys, text_values, p * slab // HEAD_DIM
        )
        returned += to_planes(contexts)
    return mix(where, planes, added, returned)


def attend(head_queries, head_keys, head_values, group_token_keys, group_tv, usable):
    query_rows = head_queries.shape[0]
    score_scale = HEAD_DIM ** (-0.5)
    reshaped_queries = head_queries.reshape(query_rows, HEADS_DEV, HEAD_DIM)

    def compute_scores(current_key_block):
        return (
            jnp.einsum(
                "qgp,ugp->gqu",
                reshaped_queries,
                current_key_block,
                preferred_element_type=jnp.float32,
            )
            * score_scale
        )

    text_scores = compute_scores(group_token_keys.reshape(-1, HEADS_DEV, HEAD_DIM))
    text_scores = jnp.where(usable[None, None, :], text_scores, -jnp.inf)
    row_top = jnp.max(text_scores, axis=-1)
    text_exp = jnp.exp(text_scores - row_top[..., None])
    denominator = jnp.sum(text_exp, axis=-1)
    weighted = jnp.einsum(
        "vie,evs->vis",
        text_exp.astype(jnp.bfloat16),
        group_tv.reshape(-1, HEADS_DEV, HEAD_DIM),
        preferred_element_type=jnp.float32,
    )
    key_total = head_keys.shape[0]
    current_key_block = 2048
    block_keys = head_keys.reshape(key_total // current_key_block, current_key_block, HEADS_DEV, HEAD_DIM)
    block_values = head_values.reshape(key_total // current_key_block, current_key_block, HEADS_DEV, HEAD_DIM)

    def advance(carry, blocks):
        old_top, old_denominator, old_weighted = carry
        local_keys, values_here = blocks
        block_scores = compute_scores(local_keys)
        new_top = jnp.maximum(old_top, jnp.max(block_scores, axis=-1))
        running_rescale = jnp.exp(old_top - new_top)
        block_exp = jnp.exp(block_scores - new_top[..., None])
        new_denominator = old_denominator * running_rescale + jnp.sum(block_exp, axis=-1)
        new_weighted = old_weighted * running_rescale[..., None] + jnp.einsum(
            "vie,evs->vis",
            block_exp.astype(jnp.bfloat16),
            values_here,
            preferred_element_type=jnp.float32,
        )
        return ((new_top, new_denominator, new_weighted), None)

    (row_top, denominator, weighted), unused = lax.scan(
        advance, (row_top, denominator, weighted), (block_keys, block_values)
    )
    context = weighted / denominator[..., None]
    return context.transpose(1, 0, 2).reshape(query_rows, HEADS_DEV * HEAD_DIM).astype(jnp.bfloat16)


def general_body(queries, keys, values, text_keys, text_values, text_len, plan, deltas):
    tok_rows, feat_width = queries.shape
    axis_count = lax.axis_size("seq")
    head_groups = HEADS // HEADS_DEV
    query_pieces = axis_count // head_groups
    slot_width = HEADS_DEV * HEAD_DIM

    def replicate_slots(array):
        spread = jnp.broadcast_to(array[:, None, :], (tok_rows, query_pieces, feat_width))
        return spread.reshape(tok_rows, query_pieces * feat_width)

    head_queries = lax.all_to_all(
        queries.reshape(tok_rows // query_pieces, query_pieces * feat_width),
        "seq",
        split_axis=1,
        concat_axis=0,
        tiled=True,
    )
    head_keys = lax.all_to_all(replicate_slots(keys), "seq", split_axis=1, concat_axis=0, tiled=True)
    head_values = lax.all_to_all(replicate_slots(values), "seq", split_axis=1, concat_axis=0, tiled=True)
    group_index = lax.axis_index("seq") % head_groups
    group_token_keys = lax.dynamic_slice_in_dim(text_keys, group_index * slot_width, slot_width, 1)
    group_tv = lax.dynamic_slice_in_dim(text_values, group_index * slot_width, slot_width, 1)
    usable = jnp.arange(text_keys.shape[0]) < text_len[0]
    context = attend(head_queries, head_keys, head_values, group_token_keys, group_tv, usable)
    returned = lax.all_to_all(context, "seq", split_axis=0, concat_axis=1, tiled=True)
    context_rows = returned.reshape(tok_rows, feat_width)
    added = (
        jnp.einsum("b,btc->tc", plan.astype(jnp.bfloat16), deltas, preferred_element_type=jnp.float32) * 0.25
    )
    return (context_rows.astype(jnp.float32) + added).astype(jnp.bfloat16)


def solution(mesh):
    size = mesh.shape["seq"]
    planes = size // PLANE
    fits = planes in (2, 4) and planes * PLANE == size and HEADS % (2 * planes) == 0
    return jax.shard_map(
        plane_body if fits else general_body,
        mesh=mesh,
        in_specs=(
            P(("grp", "seq"), None),
            P(("grp", "seq"), None),
            P(("grp", "seq"), None),
            P("grp", None),
            P("grp", None),
            P("grp"),
            P("grp"),
            P(None, ("grp", "seq"), None),
        ),
        out_specs=P(("grp", "seq"), None),
        check_vma=False,
    )
```

```python
import functools
import math

import jax
import jax.numpy as jnp
from jax import lax
from jax.experimental import pallas as pl
from jax.experimental.pallas import tpu as pltpu
from jax.sharding import PartitionSpec as P

HEADS = 24
HEAD_DIM = 128
HEADS_DEV = 3
PLANE = 4
PAIR = 2 * HEAD_DIM
EXP_SCALE = HEAD_DIM ** (-0.5) * math.log2(math.e)


def pack_kernel(spans, planes, where, *refs):
    sources, outs = refs[: len(spans)], refs[len(spans) :]
    for relative in range(planes):
        plane = jnp.bitwise_xor(where[0], relative)
        columns = pl.ds(pl.multiple_of(plane * PAIR, PAIR), PAIR)
        for slot, source in enumerate(sources):
            outs[relative][:, slot * PAIR : (slot + 1) * PAIR] = source[:, columns]


def pack(where, spans, planes):
    rows = spans[0][0].shape[0]
    slab = planes * PAIR
    shape = jax.ShapeDtypeStruct((rows, len(spans) * PAIR), spans[0][0].dtype)

    def block(phase):
        return pl.BlockSpec((rows, slab), lambda i: (0, phase))

    return pl.pallas_call(
        functools.partial(pack_kernel, spans, planes),
        grid=(1,),
        out_shape=[shape] * planes,
        in_specs=[pl.BlockSpec(memory_space=pltpu.SMEM)] + [block(phase) for _, phase in spans],
        out_specs=[pl.BlockSpec(shape.shape, lambda i: (0, 0))] * planes,
        name="pack",
    )(where, *[source for source, _ in spans])


def stack_kernel(first, n, *refs):
    pieces, out = refs[:n], refs[n]
    rows = pieces[0].shape[0]
    for index, piece in enumerate(pieces):
        out[index * rows : (index + 1) * rows] = piece[:, first:]


def stack(pieces, first):
    rows, width = pieces[0].shape
    vmem = pl.BlockSpec(memory_space=pltpu.VMEM)
    return pl.pallas_call(
        functools.partial(stack_kernel, first, len(pieces)),
        in_specs=[vmem] * len(pieces),
        out_specs=vmem,
        out_shape=jax.ShapeDtypeStruct((rows * len(pieces), width - first), pieces[0].dtype),
        name="stack",
    )(*pieces)


def attend_kernel(n_q, n_kv, scalars, *refs):
    queries = refs[:n_q]
    keys = refs[n_q : n_q + n_kv]
    values = refs[n_q + n_kv : n_q + 2 * n_kv]
    text_keys, text_values = refs[n_q + 2 * n_kv : n_q + 2 * n_kv + 2]
    outs = refs[n_q + 2 * n_kv + 2 :]
    text_slots = text_keys.shape[0]
    contract_last = (((1,), (1,)), ((), ()))
    for first in range(0, n_q, 2):
        q = jnp.concatenate([queries[first][...], queries[first + 1][...]], axis=0)
        rows = q.shape[0]
        scores = [
            lax.dot_general(q, k[...], contract_last, preferred_element_type=jnp.float32) for k in keys
        ]
        text_scores = lax.dot_general(q, text_keys[...], contract_last, preferred_element_type=jnp.float32)
        usable = lax.broadcasted_iota(jnp.int32, (rows, text_slots), 1) < scalars[1]
        scores.append(jnp.where(usable, text_scores, -jnp.inf))
        top = functools.reduce(jnp.maximum, [jnp.max(s, axis=1, keepdims=True) for s in scores])
        total = jnp.zeros((rows, 1), jnp.float32)
        weighted = jnp.zeros((rows, HEAD_DIM), jnp.float32)
        for s, v in zip(scores, (*values, text_values)):
            weights = jnp.exp2((s - top) * EXP_SCALE)
            total = total + jnp.sum(weights, axis=1, keepdims=True)
            weighted = weighted + jnp.dot(
                weights.astype(jnp.bfloat16), v[...], preferred_element_type=jnp.float32
            )
        context = (weighted / total).astype(jnp.bfloat16)
        half = rows // 2
        outs[first][...] = context[:half]
        outs[first + 1][...] = context[half:]


def attend_pair(scalars, queries, q_block, kvs, text_keys, text_values, text_block):
    n_q, n_kv = len(queries), len(kvs)
    rows = queries[0].shape[0]
    slots = text_keys.shape[0]

    def column(block):
        return lambda head, scalars: (0, block + head)

    def text_column(head, scalars):
        return (0, text_block + scalars[0] * 2 + head)

    in_specs = [pl.BlockSpec((rows, HEAD_DIM), column(q_block)) for _ in queries]
    in_specs += [pl.BlockSpec((kv.shape[0], HEAD_DIM), column(0)) for kv in kvs]
    in_specs += [pl.BlockSpec((kv.shape[0], HEAD_DIM), column(2)) for kv in kvs]
    in_specs += [pl.BlockSpec((slots, HEAD_DIM), text_column)] * 2
    n_keys = sum(kv.shape[0] for kv in kvs) + slots
    work = 2 * n_q * rows * n_keys
    return pl.pallas_call(
        functools.partial(attend_kernel, n_q, n_kv),
        grid_spec=pltpu.PrefetchScalarGridSpec(
            num_scalar_prefetch=1,
            grid=(2,),
            in_specs=in_specs,
            out_specs=[pl.BlockSpec((rows, HEAD_DIM), column(0)) for _ in queries],
        ),
        out_shape=[jax.ShapeDtypeStruct((rows, PAIR), jnp.bfloat16)] * n_q,
        compiler_params=pltpu.CompilerParams(vmem_limit_bytes=40 * 1024 * 1024),
        cost_estimate=pl.CostEstimate(
            flops=work * HEAD_DIM * 4, bytes_accessed=4 * n_keys * PAIR, transcendentals=work
        ),
        name="attend",
    )(scalars, *queries, *kvs, *kvs, text_keys, text_values)


def deltas_kernel(plan, deltas, out):
    total = plan[0].astype(jnp.float32) * deltas[0].astype(jnp.float32)
    for block in range(1, deltas.shape[0]):
        total = total + plan[block].astype(jnp.float32) * deltas[block].astype(jnp.float32)
    out[...] = total * 0.25


def sum_deltas(plan, deltas):
    blocks, rows, width = deltas.shape
    step = width // 4
    return pl.pallas_call(
        deltas_kernel,
        grid=(4,),
        in_specs=[
            pl.BlockSpec(memory_space=pltpu.SMEM),
            pl.BlockSpec((blocks, rows, step), lambda i: (0, 0, i)),
        ],
        out_specs=pl.BlockSpec((rows, step), lambda i: (0, i)),
        out_shape=jax.ShapeDtypeStruct((rows, width), jnp.float32),
        cost_estimate=pl.CostEstimate(
            flops=2 * blocks * rows * width, bytes_accessed=2 * blocks * rows * width, transcendentals=0
        ),
        name="deltas",
    )(plan, deltas)


def mix_kernel(planes, where, added, *refs):
    pieces, out = refs[:-1], refs[-1]
    slab = planes * PAIR
    for index, piece in enumerate(pieces):
        phase, relative = divmod(index, planes)
        plane = jnp.bitwise_xor(where[0], relative)
        columns = pl.ds(pl.multiple_of(phase * slab + plane * PAIR, PAIR), PAIR)
        out[:, columns] = (piece[...].astype(jnp.float32) + added[:, columns]).astype(out.dtype)


def mix(where, planes, added, pieces):
    vmem = pl.BlockSpec(memory_space=pltpu.VMEM)
    return pl.pallas_call(
        functools.partial(mix_kernel, planes),
        in_specs=[pl.BlockSpec(memory_space=pltpu.SMEM)] + [vmem] * (1 + len(pieces)),
        out_specs=vmem,
        out_shape=jax.ShapeDtypeStruct(added.shape, jnp.bfloat16),
        name="mix",
    )(where, added, *pieces)


def plane_body(queries, keys, values, text_keys, text_values, text_len, plan, deltas):
    size = lax.axis_size("seq")
    planes = size // PLANE
    slab = planes * PAIR
    phases = HEADS * HEAD_DIM // slab
    plane = lax.axis_index("seq") // PLANE
    where = plane.astype(jnp.int32).reshape(1)
    scalars = jnp.concatenate([where, text_len])

    def swap(array, distance):
        return lax.ppermute(array, "seq", [(i, i ^ distance) for i in range(size)])

    def to_planes(pieces):
        return [pieces[0]] + [swap(pieces[r], PLANE * r) for r in range(1, planes)]

    def gather_plane(pieces, first):
        own = stack(pieces, first)
        other = swap(own, 2)
        return [own, other, swap(own, 1), swap(other, 1)]

    first = to_planes(pack(where, ((queries, 0), (keys, 0), (values, 0)), planes))
    rest = [
        to_planes(pack(where, ((keys, p), (values, p)), planes)) for p in range(1, phases)
    ]
    later = to_planes(pack(where, [(queries, p) for p in range(1, phases)], planes))

    gathered = [gather_plane(first, PAIR)] + [gather_plane(pieces, 0) for pieces in rest]
    added = sum_deltas(plan, deltas)
    returned = []
    for p in range(phases):
        pieces, block = (first, 0) if p == 0 else (later, 2 * (p - 1))
        contexts = attend_pair(
            scalars, pieces, block, gathered[p], text_keys, text_values, p * slab // HEAD_DIM
        )
        returned += to_planes(contexts)
    return mix(where, planes, added, returned)


def attend(head_queries, head_keys, head_values, group_token_keys, group_tv, usable):
    query_rows = head_queries.shape[0]
    score_scale = HEAD_DIM ** (-0.5)
    reshaped_queries = head_queries.reshape(query_rows, HEADS_DEV, HEAD_DIM)

    def compute_scores(current_key_block):
        return (
            jnp.einsum(
                "qgp,ugp->gqu",
                reshaped_queries,
                current_key_block,
                preferred_element_type=jnp.float32,
            )
            * score_scale
        )

    text_scores = compute_scores(group_token_keys.reshape(-1, HEADS_DEV, HEAD_DIM))
    text_scores = jnp.where(usable[None, None, :], text_scores, -jnp.inf)
    row_top = jnp.max(text_scores, axis=-1)
    text_exp = jnp.exp(text_scores - row_top[..., None])
    denominator = jnp.sum(text_exp, axis=-1)
    weighted = jnp.einsum(
        "vie,evs->vis",
        text_exp.astype(jnp.bfloat16),
        group_tv.reshape(-1, HEADS_DEV, HEAD_DIM),
        preferred_element_type=jnp.float32,
    )
    key_total = head_keys.shape[0]
    current_key_block = 2048
    block_keys = head_keys.reshape(key_total // current_key_block, current_key_block, HEADS_DEV, HEAD_DIM)
    block_values = head_values.reshape(key_total // current_key_block, current_key_block, HEADS_DEV, HEAD_DIM)

    def advance(carry, blocks):
        old_top, old_denominator, old_weighted = carry
        local_keys, values_here = blocks
        block_scores = compute_scores(local_keys)
        new_top = jnp.maximum(old_top, jnp.max(block_scores, axis=-1))
        running_rescale = jnp.exp(old_top - new_top)
        block_exp = jnp.exp(block_scores - new_top[..., None])
        new_denominator = old_denominator * running_rescale + jnp.sum(block_exp, axis=-1)
        new_weighted = old_weighted * running_rescale[..., None] + jnp.einsum(
            "vie,evs->vis",
            block_exp.astype(jnp.bfloat16),
            values_here,
            preferred_element_type=jnp.float32,
        )
        return ((new_top, new_denominator, new_weighted), None)

    (row_top, denominator, weighted), unused = lax.scan(
        advance, (row_top, denominator, weighted), (block_keys, block_values)
    )
    context = weighted / denominator[..., None]
    return context.transpose(1, 0, 2).reshape(query_rows, HEADS_DEV * HEAD_DIM).astype(jnp.bfloat16)


def general_body(queries, keys, values, text_keys, text_values, text_len, plan, deltas):
    tok_rows, feat_width = queries.shape
    axis_count = lax.axis_size("seq")
    head_groups = HEADS // HEADS_DEV
    query_pieces = axis_count // head_groups
    slot_width = HEADS_DEV * HEAD_DIM

    def replicate_slots(array):
        spread = jnp.broadcast_to(array[:, None, :], (tok_rows, query_pieces, feat_width))
        return spread.reshape(tok_rows, query_pieces * feat_width)

    head_queries = lax.all_to_all(
        queries.reshape(tok_rows // query_pieces, query_pieces * feat_width),
        "seq",
        split_axis=1,
        concat_axis=0,
        tiled=True,
    )
    head_keys = lax.all_to_all(replicate_slots(keys), "seq", split_axis=1, concat_axis=0, tiled=True)
    head_values = lax.all_to_all(replicate_slots(values), "seq", split_axis=1, concat_axis=0, tiled=True)
    group_index = lax.axis_index("seq") % head_groups
    group_token_keys = lax.dynamic_slice_in_dim(text_keys, group_index * slot_width, slot_width, 1)
    group_tv = lax.dynamic_slice_in_dim(text_values, group_index * slot_width, slot_width, 1)
    usable = jnp.arange(text_keys.shape[0]) < text_len[0]
    context = attend(head_queries, head_keys, head_values, group_token_keys, group_tv, usable)
    returned = lax.all_to_all(context, "seq", split_axis=0, concat_axis=1, tiled=True)
    context_rows = returned.reshape(tok_rows, feat_width)
    added = (
        jnp.einsum("b,btc->tc", plan.astype(jnp.bfloat16), deltas, preferred_element_type=jnp.float32) * 0.25
    )
    return (context_rows.astype(jnp.float32) + added).astype(jnp.bfloat16)


def solution(mesh):
    size = mesh.shape["seq"]
    planes = size // PLANE
    fits = planes in (2, 4) and planes * PLANE == size and HEADS % (2 * planes) == 0
    return jax.shard_map(
        plane_body if fits else general_body,
        mesh=mesh,
        in_specs=(
            P(("grp", "seq"), None),
            P(("grp", "seq"), None),
            P(("grp", "seq"), None),
            P("grp", None),
            P("grp", None),
            P("grp"),
            P("grp"),
            P(None, ("grp", "seq"), None),
        ),
        out_specs=P(("grp", "seq"), None),
        check_vma=False,
    )
```

```python
import functools
import math

import jax
import jax.numpy as jnp
from jax import lax
from jax.experimental import pallas as pl
from jax.experimental.pallas import tpu as pltpu
from jax.sharding import PartitionSpec as P

HEADS = 24
HEAD_DIM = 128
HEADS_DEV = 3
PLANE = 4
PAIR = 2 * HEAD_DIM
EXP_SCALE = HEAD_DIM ** (-0.5) * math.log2(math.e)


SMALL = pl.CostEstimate(flops=1, bytes_accessed=1, transcendentals=0)
LARGE = pl.CostEstimate(flops=20000000000, bytes_accessed=1, transcendentals=0)
MID = pl.CostEstimate(flops=1000000000, bytes_accessed=1, transcendentals=0)


def first_pack_kernel(spans, planes, where, *refs):
    sources, outs = refs[: len(spans)], refs[len(spans) : len(spans) + planes]
    slabs, sems = refs[-2:]
    copies = [
        pltpu.make_async_copy(source.at[:, pl.ds(phase * planes * PAIR, planes * PAIR)], slabs.at[slot], sems.at[slot])
        for slot, (source, phase) in enumerate(zip(sources, spans))
    ]
    for copy in copies:
        copy.start()
    for copy in copies:
        copy.wait()
    for relative, out in enumerate(outs):
        plane = jnp.bitwise_xor(where[0], relative)
        columns = pl.ds(pl.multiple_of(plane * PAIR, PAIR), PAIR)
        for slot in range(len(spans)):
            out[:, slot * PAIR : (slot + 1) * PAIR] = slabs[slot, :, columns]


def first_pack(where, phase, planes, *sources):
    rows = sources[0].shape[0]
    vmem = pl.BlockSpec(memory_space=pltpu.VMEM)
    return pl.pallas_call(
        functools.partial(first_pack_kernel, [phase] * len(sources), planes),
        out_shape=[jax.ShapeDtypeStruct((rows, len(sources) * PAIR), sources[0].dtype)] * planes,
        in_specs=[pl.BlockSpec(memory_space=pltpu.SMEM)] + [pl.BlockSpec(memory_space=pltpu.HBM)] * len(sources),
        out_specs=[vmem] * planes,
        scratch_shapes=[
            pltpu.VMEM((len(sources), rows, planes * PAIR), sources[0].dtype),
            pltpu.SemaphoreType.DMA((len(sources),)),
        ],
        compiler_params=pltpu.CompilerParams(vmem_limit_bytes=4 * 2**20),
        cost_estimate=SMALL,
        name="first_pack",
    )(where, *sources)


def pack_kernel(groups, planes, n_out, where, *refs):
    sources, outs = refs[:3], refs[-n_out:]
    slab = planes * PAIR
    for relative in range(planes):
        plane = jnp.bitwise_xor(where[0], relative)
        for index, spans in enumerate(groups):
            out = outs[index * planes + relative]
            for slot, (source, phase) in enumerate(spans):
                columns = pl.ds(pl.multiple_of(phase * slab + plane * PAIR, PAIR), PAIR)
                out[:, slot * PAIR : (slot + 1) * PAIR] = sources[source][:, columns]


def pack(where, groups, planes, sources, earlier):
    rows = sources[0].shape[0]
    shapes = [
        jax.ShapeDtypeStruct((rows, len(spans) * PAIR), sources[0].dtype) for spans in groups for _ in range(planes)
    ]
    vmem = pl.BlockSpec(memory_space=pltpu.VMEM)
    outs = pl.pallas_call(
        functools.partial(pack_kernel, groups, planes, len(shapes)),
        out_shape=shapes,
        in_specs=[pl.BlockSpec(memory_space=pltpu.SMEM)]
        + [vmem] * len(sources)
        + [pl.BlockSpec(memory_space=pl.ANY)] * len(earlier),
        out_specs=[vmem] * len(shapes),
        compiler_params=pltpu.CompilerParams(vmem_limit_bytes=8 * 2**20),
        cost_estimate=SMALL,
        name="pack",
    )(where, *sources, *earlier)
    return [outs[i * planes : (i + 1) * planes] for i in range(len(groups))]


def tick_kernel(axes, counts, widths, n_earlier, *refs):
    sources, outs = list(refs[n_earlier : n_earlier + sum(counts)]), refs[n_earlier + sum(counts) :]
    for axis, count, width, out in zip(axes, counts, widths, outs):
        at = 0
        for _ in range(count):
            source = sources.pop(0)
            if axis == 0:
                out[at : at + source.shape[0]] = source[:, :width]
                at += source.shape[0]
            else:
                out[:, at : at + source.shape[1]] = source[...]
                at += source.shape[1]


def tick(jobs, earlier, cost):
    axes = [axis for axis, _, _ in jobs]
    counts = [len(arrays) for _, arrays, _ in jobs]
    widths = [width or arrays[0].shape[1] for _, arrays, width in jobs]
    shapes = []
    for axis, arrays, width in jobs:
        if axis == 0:
            shape = (sum(a.shape[0] for a in arrays), width or arrays[0].shape[1])
        else:
            shape = (arrays[0].shape[0], sum(a.shape[1] for a in arrays))
        shapes.append(jax.ShapeDtypeStruct(shape, jnp.bfloat16))
    vmem = pl.BlockSpec(memory_space=pltpu.VMEM)
    return pl.pallas_call(
        functools.partial(tick_kernel, axes, counts, widths, len(earlier)),
        in_specs=[pl.BlockSpec(memory_space=pl.ANY)] * len(earlier) + [vmem] * sum(counts),
        out_specs=[vmem] * len(shapes),
        out_shape=shapes,
        compiler_params=pltpu.CompilerParams(vmem_limit_bytes=6 * 2**20),
        cost_estimate=cost,
        name="tick",
    )(*earlier, *[a for _, arrays, _ in jobs for a in arrays])


def attend_kernel(n_q, n_kv, q_column, text_column, scalars, *refs):
    queries, kvs = refs[:n_q], refs[n_q : n_q + n_kv]
    text_keys, text_values = refs[n_q + n_kv : n_q + n_kv + 2]
    outs = refs[len(refs) - n_q :]
    rows = outs[0].shape[0]
    contract_last = (((1,), (1,)), ((), ()))
    for head in range(2):
        here = slice(head * HEAD_DIM, (head + 1) * HEAD_DIM)
        over = slice(PAIR + head * HEAD_DIM, PAIR + (head + 1) * HEAD_DIM)
        text = slice(text_column + head * HEAD_DIM, text_column + (head + 1) * HEAD_DIM)
        q_here = slice(q_column + head * HEAD_DIM, q_column + (head + 1) * HEAD_DIM)
        q = jnp.concatenate([piece[:, q_here] for piece in queries], axis=0)
        blocks = [(kv[:, here], kv[:, over]) for kv in kvs] + [(text_keys[:, text], text_values[:, text])]
        top = None
        for index, (keys, values) in enumerate(blocks):
            scores = lax.dot_general(q, keys, contract_last, preferred_element_type=jnp.float32)
            if index == n_kv:
                usable = lax.broadcasted_iota(jnp.int32, scores.shape, 1) < scalars[1]
                scores = jnp.where(usable, scores, -jnp.inf)
            block_top = jnp.max(scores, axis=1, keepdims=True)
            new_top = block_top if top is None else jnp.maximum(top, block_top)
            weights = jnp.exp2((scores - new_top) * EXP_SCALE)
            block_total = jnp.sum(weights, axis=1, keepdims=True)
            block_weighted = jnp.dot(weights.astype(jnp.bfloat16), values, preferred_element_type=jnp.float32)
            if top is None:
                total, weighted = block_total, block_weighted
            else:
                rescale = jnp.exp2((top - new_top) * EXP_SCALE)
                total, weighted = total * rescale + block_total, weighted * rescale + block_weighted
            top = new_top
        context = (weighted / total).astype(jnp.bfloat16)
        for index, out in enumerate(outs):
            out[:, here] = context[index * rows : (index + 1) * rows]


def attend_pair(scalars, queries, q_block, kvs, text_keys, text_values, text_block, earlier):
    n_q, n_kv = len(queries), len(kvs)
    vmem = pl.BlockSpec(memory_space=pltpu.VMEM)
    return pl.pallas_call(
        functools.partial(attend_kernel, n_q, n_kv, q_block * HEAD_DIM, text_block * HEAD_DIM),
        in_specs=[pl.BlockSpec(memory_space=pltpu.SMEM)]
        + [vmem] * (n_q + n_kv + 2)
        + [pl.BlockSpec(memory_space=pl.ANY)] * len(earlier),
        out_specs=[vmem] * n_q,
        out_shape=[jax.ShapeDtypeStruct((queries[0].shape[0], PAIR), jnp.bfloat16)] * n_q,
        compiler_params=pltpu.CompilerParams(vmem_limit_bytes=24 * 2**20),
        cost_estimate=SMALL,
        name="attend",
    )(scalars, *queries, *kvs, text_keys, text_values, *earlier)


def text_kernel(planes, where, keys, values, *refs):
    keys_out, values_out = refs[-2:]
    slab = planes * PAIR
    for phase in range(keys.shape[1] // slab):
        columns = pl.ds(pl.multiple_of(phase * slab + where[0] * PAIR, PAIR), PAIR)
        keys_out[:, phase * PAIR : (phase + 1) * PAIR] = keys[:, columns]
        values_out[:, phase * PAIR : (phase + 1) * PAIR] = values[:, columns]


def own_text(where, planes, text_keys, text_values, earlier):
    vmem = pl.BlockSpec(memory_space=pltpu.VMEM)
    shape = jax.ShapeDtypeStruct((text_keys.shape[0], text_keys.shape[1] // planes), text_keys.dtype)
    return pl.pallas_call(
        functools.partial(text_kernel, planes),
        in_specs=[pl.BlockSpec(memory_space=pltpu.SMEM), vmem, vmem]
        + [pl.BlockSpec(memory_space=pl.ANY)] * len(earlier),
        out_specs=[vmem] * 2,
        out_shape=[shape] * 2,
        compiler_params=pltpu.CompilerParams(vmem_limit_bytes=6 * 2**20),
        cost_estimate=SMALL,
        name="own_text",
    )(where, text_keys, text_values, *earlier)


def deltas_kernel(plan, deltas, *refs):
    out = refs[-1]
    total = plan[0].astype(jnp.float32) * deltas[0].astype(jnp.float32)
    for block in range(1, deltas.shape[0]):
        total = total + plan[block].astype(jnp.float32) * deltas[block].astype(jnp.float32)
    out[...] = total * 0.25


def sum_deltas(plan, deltas, earlier):
    blocks, rows, width = deltas.shape
    step = width // 4
    return pl.pallas_call(
        deltas_kernel,
        grid=(4,),
        in_specs=[
            pl.BlockSpec(memory_space=pltpu.SMEM),
            pl.BlockSpec((blocks, rows, step), lambda i: (0, 0, i)),
        ]
        + [pl.BlockSpec(memory_space=pl.ANY)] * len(earlier),
        out_specs=pl.BlockSpec((rows, step), lambda i: (0, i)),
        out_shape=jax.ShapeDtypeStruct((rows, width), jnp.float32),
        cost_estimate=SMALL,
        compiler_params=pltpu.CompilerParams(vmem_limit_bytes=6 * 2**20),
        name="deltas",
    )(plan, deltas, *earlier)


def mix_kernel(planes, where, added, *refs):
    pieces, out = refs[:-1], refs[-1]
    slab = planes * PAIR
    phase = 0
    for first in range(0, len(pieces), planes):
        for part in range(pieces[first].shape[1] // PAIR):
            for relative in range(planes):
                plane = jnp.bitwise_xor(where[0], relative)
                columns = pl.ds(pl.multiple_of(phase * slab + plane * PAIR, PAIR), PAIR)
                piece = pieces[first + relative][:, part * PAIR : (part + 1) * PAIR]
                out[:, columns] = (piece.astype(jnp.float32) + added[:, columns]).astype(out.dtype)
            phase += 1


def mix(where, planes, added, pieces):
    vmem = pl.BlockSpec(memory_space=pltpu.VMEM)
    return pl.pallas_call(
        functools.partial(mix_kernel, planes),
        in_specs=[pl.BlockSpec(memory_space=pltpu.SMEM)] + [vmem] * (1 + len(pieces)),
        out_specs=vmem,
        out_shape=jax.ShapeDtypeStruct(added.shape, jnp.bfloat16),
        compiler_params=pltpu.CompilerParams(vmem_limit_bytes=6 * 2**20),
        cost_estimate=SMALL,
        name="mix",
    )(where, added, *pieces)


def plane_body(queries, keys, values, text_keys, text_values, text_len, plan, deltas):
    size = lax.axis_size("seq")
    planes = size // PLANE
    slab = planes * PAIR
    plane = lax.axis_index("seq") // PLANE
    where = plane.astype(jnp.int32).reshape(1)
    scalars = jnp.concatenate([where, text_len])

    def swap(array, distance):
        return lax.ppermute(array, "seq", [(i, i ^ distance) for i in range(size)])

    def send(piece, r):
        return swap(piece, PLANE * r)

    def heads(p, pieces, block, gathered, earlier):
        return attend_pair(
            scalars, pieces, block, gathered, text_keys, text_values, 2 * p, earlier
        )

    fast, slow = (3,), (1, 2)
    z1 = first_pack(where, 0, planes, keys, values)
    groups = [((1, 1), (2, 1)), ((1, 2), (2, 2), (0, 0)), ((0, 1),), ((0, 2),)]
    z2, z3, z4, z5 = pack(where, groups, planes, (queries, keys, values), z1)
    text_keys, text_values = own_text(where, planes, text_keys, text_values, [z5[0]])
    added = sum_deltas(plan, deltas, [text_keys])

    def release(batch, lanes):
        return [(0, [batch[r]], None) for r in lanes]

    in1 = {r: send(z1[r], r) for r in range(1, planes)}
    out = tick(release(z2, fast), [in1[r] for r in fast] + [added], LARGE)
    in2 = {r: send(piece, r) for r, piece in zip(fast, out)}
    out = tick([(0, [z1[0]] + [in1[r] for r in range(1, planes)], 2 * PAIR)] + release(z2, slow), [out[0]], MID)
    own1, sent = out[0], out[1:]
    other1 = swap(own1, 2)
    in2.update({r: send(piece, r) for r, piece in zip(slow, sent)})
    out = tick(release(z3, fast), [in2[r] for r in fast] + [own1], LARGE)
    in3 = {r: send(piece, r) for r, piece in zip(fast, out)}
    out = tick(
        [(0, [other1, own1], None), (0, [z2[0]] + [in2[r] for r in range(1, planes)], 2 * PAIR)] + release(z3, slow),
        [out[0]],
        MID,
    )
    pair1, own2, sent = out[0], out[1], out[2:]
    other2, core1 = swap(own2, 2), swap(pair1, 1)
    in3.update({r: send(piece, r) for r, piece in zip(slow, sent)})
    out = tick(release(z4, fast), [own2] + [in3[r] for r in fast], LARGE)
    in4 = {r: send(piece, r) for r, piece in zip(fast, out)}
    out = tick(
        [(0, [other2, own2], None), (0, [z3[0]] + [in3[r] for r in range(1, planes)], 2 * PAIR)] + release(z4, slow),
        [in3[r] for r in slow] + [out[0]],
        MID,
    )
    pair2, own3, sent = out[0], out[1], out[2:]
    other3, core2 = swap(own3, 2), swap(pair2, 1)
    in4.update({r: send(piece, r) for r, piece in zip(slow, sent)})
    context1 = heads(0, [z3[0]] + [in3[r] for r in range(1, planes)], 4, [pair1, core1], [own3])
    out = tick(release(z5, fast), [context1[0]] + [in4[r] for r in fast], LARGE)
    in5 = {r: send(piece, r) for r, piece in zip(fast, out)}
    out = tick(release(z5, slow), [in4[r] for r in slow] + [out[0]], MID)
    in5.update({r: send(piece, r) for r, piece in zip(slow, out)})
    context2 = heads(1, [z4[0]] + [in4[r] for r in range(1, planes)], 0, [pair2, core2], [out[0]])
    out = tick([(0, [other3, own3], None)] + [(1, [context1[r], context2[r]], None) for r in range(planes)], [in5[r] for r in range(1, planes)], MID)
    pair3, contexts = out[0], out[1:]
    core3 = swap(pair3, 1)
    returned = [contexts[0]] + [send(contexts[r], r) for r in range(1, planes)]
    context3 = heads(2, [z5[0]] + [in5[r] for r in range(1, planes)], 0, [pair3, core3], [])
    returned += [context3[0]] + [send(context3[r], r) for r in range(1, planes)]
    return mix(where, planes, added, returned)


def attend(head_queries, head_keys, head_values, group_token_keys, group_tv, usable):
    query_rows = head_queries.shape[0]
    score_scale = HEAD_DIM ** (-0.5)
    reshaped_queries = head_queries.reshape(query_rows, HEADS_DEV, HEAD_DIM)

    def compute_scores(current_key_block):
        return (
            jnp.einsum(
                "qgp,ugp->gqu",
                reshaped_queries,
                current_key_block,
                preferred_element_type=jnp.float32,
            )
            * score_scale
        )

    text_scores = compute_scores(group_token_keys.reshape(-1, HEADS_DEV, HEAD_DIM))
    text_scores = jnp.where(usable[None, None, :], text_scores, -jnp.inf)
    row_top = jnp.max(text_scores, axis=-1)
    text_exp = jnp.exp(text_scores - row_top[..., None])
    denominator = jnp.sum(text_exp, axis=-1)
    weighted = jnp.einsum(
        "vie,evs->vis",
        text_exp.astype(jnp.bfloat16),
        group_tv.reshape(-1, HEADS_DEV, HEAD_DIM),
        preferred_element_type=jnp.float32,
    )
    key_total = head_keys.shape[0]
    current_key_block = 2048
    block_keys = head_keys.reshape(key_total // current_key_block, current_key_block, HEADS_DEV, HEAD_DIM)
    block_values = head_values.reshape(key_total // current_key_block, current_key_block, HEADS_DEV, HEAD_DIM)

    def advance(carry, blocks):
        old_top, old_denominator, old_weighted = carry
        local_keys, values_here = blocks
        block_scores = compute_scores(local_keys)
        new_top = jnp.maximum(old_top, jnp.max(block_scores, axis=-1))
        running_rescale = jnp.exp(old_top - new_top)
        block_exp = jnp.exp(block_scores - new_top[..., None])
        new_denominator = old_denominator * running_rescale + jnp.sum(block_exp, axis=-1)
        new_weighted = old_weighted * running_rescale[..., None] + jnp.einsum(
            "vie,evs->vis",
            block_exp.astype(jnp.bfloat16),
            values_here,
            preferred_element_type=jnp.float32,
        )
        return ((new_top, new_denominator, new_weighted), None)

    (row_top, denominator, weighted), unused = lax.scan(
        advance, (row_top, denominator, weighted), (block_keys, block_values)
    )
    context = weighted / denominator[..., None]
    return context.transpose(1, 0, 2).reshape(query_rows, HEADS_DEV * HEAD_DIM).astype(jnp.bfloat16)


def general_body(queries, keys, values, text_keys, text_values, text_len, plan, deltas):
    tok_rows, feat_width = queries.shape
    axis_count = lax.axis_size("seq")
    head_groups = HEADS // HEADS_DEV
    query_pieces = axis_count // head_groups
    slot_width = HEADS_DEV * HEAD_DIM

    def replicate_slots(array):
        spread = jnp.broadcast_to(array[:, None, :], (tok_rows, query_pieces, feat_width))
        return spread.reshape(tok_rows, query_pieces * feat_width)

    head_queries = lax.all_to_all(
        queries.reshape(tok_rows // query_pieces, query_pieces * feat_width),
        "seq",
        split_axis=1,
        concat_axis=0,
        tiled=True,
    )
    head_keys = lax.all_to_all(replicate_slots(keys), "seq", split_axis=1, concat_axis=0, tiled=True)
    head_values = lax.all_to_all(replicate_slots(values), "seq", split_axis=1, concat_axis=0, tiled=True)
    group_index = lax.axis_index("seq") % head_groups
    group_token_keys = lax.dynamic_slice_in_dim(text_keys, group_index * slot_width, slot_width, 1)
    group_tv = lax.dynamic_slice_in_dim(text_values, group_index * slot_width, slot_width, 1)
    usable = jnp.arange(text_keys.shape[0]) < text_len[0]
    context = attend(head_queries, head_keys, head_values, group_token_keys, group_tv, usable)
    returned = lax.all_to_all(context, "seq", split_axis=0, concat_axis=1, tiled=True)
    context_rows = returned.reshape(tok_rows, feat_width)
    added = (
        jnp.einsum("b,btc->tc", plan.astype(jnp.bfloat16), deltas, preferred_element_type=jnp.float32) * 0.25
    )
    return (context_rows.astype(jnp.float32) + added).astype(jnp.bfloat16)


def solution(mesh):
    size = mesh.shape["seq"]
    planes = size // PLANE
    fits = planes in (2, 4) and planes * PLANE == size and HEADS % (2 * planes) == 0
    return jax.shard_map(
        plane_body if fits else general_body,
        mesh=mesh,
        in_specs=(
            P(("grp", "seq"), None),
            P(("grp", "seq"), None),
            P(("grp", "seq"), None),
            P("grp", None),
            P("grp", None),
            P("grp"),
            P("grp"),
            P(None, ("grp", "seq"), None),
        ),
        out_specs=P(("grp", "seq"), None),
        check_vma=False,
    )
```

```python
import functools
import math

import jax
import jax.numpy as jnp
from jax import lax
from jax.experimental import pallas as pl
from jax.experimental.pallas import tpu as pltpu
from jax.sharding import PartitionSpec as P

HEADS = 24
HEAD_DIM = 128
HEADS_DEV = 3
PLANE = 4
PAIR = 2 * HEAD_DIM
EXP_SCALE = HEAD_DIM ** (-0.5) * math.log2(math.e)


SMALL = pl.CostEstimate(flops=1, bytes_accessed=1, transcendentals=0)
MID = pl.CostEstimate(flops=10**9, bytes_accessed=1, transcendentals=0)
BIG = pl.CostEstimate(flops=2 * 10**10, bytes_accessed=1, transcendentals=0)


def first_pack_kernel(planes, where, keys, values, *refs):
    outs, own = refs[:planes], refs[planes]
    slab = planes * PAIR
    for slot, source in enumerate((keys, values)):
        here = slice(slot * PAIR, (slot + 1) * PAIR)
        for relative, out in enumerate(outs):
            plane = jnp.bitwise_xor(where[0], relative)
            out[:, here] = source[:, pl.ds(pl.multiple_of(plane * PAIR, PAIR), PAIR)]
        for phase in range(keys.shape[1] // slab):
            start = pl.multiple_of(phase * slab + where[0] * PAIR, PAIR)
            at = (2 * phase + slot) * PAIR
            own[:, at : at + PAIR] = source[:, pl.ds(start, PAIR)]


def first_pack(where, planes, keys, values):
    rows, width = keys.shape
    vmem = pl.BlockSpec(memory_space=pltpu.VMEM)
    shapes = [jax.ShapeDtypeStruct((rows, 2 * PAIR), keys.dtype)] * planes
    shapes.append(jax.ShapeDtypeStruct((rows, 2 * width // planes), keys.dtype))
    return pl.pallas_call(
        functools.partial(first_pack_kernel, planes),
        out_shape=shapes,
        in_specs=[pl.BlockSpec(memory_space=pltpu.SMEM), vmem, vmem],
        out_specs=[vmem] * len(shapes),
        compiler_params=pltpu.CompilerParams(vmem_limit_bytes=6 * 2**20),
        cost_estimate=SMALL,
        name="first_pack",
    )(where, keys, values)


def pack_kernel(groups, planes, n_out, where, *refs):
    sources, outs = refs[:3], refs[-n_out:]
    slab = planes * PAIR
    for relative in range(planes):
        plane = jnp.bitwise_xor(where[0], relative)
        for index, spans in enumerate(groups):
            out = outs[index * planes + relative]
            for slot, (source, phase) in enumerate(spans):
                columns = pl.ds(pl.multiple_of(phase * slab + plane * PAIR, PAIR), PAIR)
                out[:, slot * PAIR : (slot + 1) * PAIR] = sources[source][:, columns]


def pack(where, groups, planes, sources, earlier):
    rows = sources[0].shape[0]
    shapes = [
        jax.ShapeDtypeStruct((rows, len(spans) * PAIR), sources[0].dtype) for spans in groups for _ in range(planes)
    ]
    vmem = pl.BlockSpec(memory_space=pltpu.VMEM)
    outs = pl.pallas_call(
        functools.partial(pack_kernel, groups, planes, len(shapes)),
        out_shape=shapes,
        in_specs=[pl.BlockSpec(memory_space=pltpu.SMEM)]
        + [vmem] * len(sources)
        + [pl.BlockSpec(memory_space=pl.ANY)] * len(earlier),
        out_specs=[vmem] * len(shapes),
        compiler_params=pltpu.CompilerParams(vmem_limit_bytes=8 * 2**20),
        cost_estimate=SMALL,
        name="pack",
    )(where, *sources, *earlier)
    return [outs[i * planes : (i + 1) * planes] for i in range(len(groups))]


def tick_kernel(axes, counts, widths, n_earlier, *refs):
    sources, outs = list(refs[n_earlier : n_earlier + sum(counts)]), refs[n_earlier + sum(counts) :]
    for axis, count, width, out in zip(axes, counts, widths, outs):
        at = 0
        for _ in range(count):
            source = sources.pop(0)
            if axis == 0:
                out[at : at + source.shape[0]] = source[:, :width]
                at += source.shape[0]
            else:
                out[:, at : at + source.shape[1]] = source[...]
                at += source.shape[1]


def tick(jobs, earlier, cost):
    axes = [axis for axis, _, _ in jobs]
    counts = [len(arrays) for _, arrays, _ in jobs]
    widths = [width or arrays[0].shape[1] for _, arrays, width in jobs]
    shapes = []
    for axis, arrays, width in jobs:
        if axis == 0:
            shape = (sum(a.shape[0] for a in arrays), width or arrays[0].shape[1])
        else:
            shape = (arrays[0].shape[0], sum(a.shape[1] for a in arrays))
        shapes.append(jax.ShapeDtypeStruct(shape, jnp.bfloat16))
    vmem = pl.BlockSpec(memory_space=pltpu.VMEM)
    return pl.pallas_call(
        functools.partial(tick_kernel, axes, counts, widths, len(earlier)),
        in_specs=[pl.BlockSpec(memory_space=pl.ANY)] * len(earlier) + [vmem] * sum(counts),
        out_specs=[vmem] * len(shapes),
        out_shape=shapes,
        compiler_params=pltpu.CompilerParams(vmem_limit_bytes=6 * 2**20),
        cost_estimate=cost,
        name="tick",
    )(*earlier, *[a for _, arrays, _ in jobs for a in arrays])


def attend_kernel(n_q, q_column, groups, scalars, *refs):
    queries, outs = refs[:n_q], refs[len(refs) - n_q :]
    arrays = refs[n_q:]
    rows = outs[0].shape[0]
    contract_last = (((1,), (1,)), ((), ()))

    def columns(group, head, which):
        parts = []
        for index, key_column, value_column in group:
            start = (value_column if which else key_column) + head * HEAD_DIM
            parts.append(arrays[index][:, start : start + HEAD_DIM])
        return parts[0] if len(parts) == 1 else jnp.concatenate(parts, axis=0)

    for head in range(2):
        here = slice(head * HEAD_DIM, (head + 1) * HEAD_DIM)
        q_here = slice(q_column + head * HEAD_DIM, q_column + (head + 1) * HEAD_DIM)
        q = jnp.concatenate([piece[:, q_here] for piece in queries], axis=0)
        top = None
        for number, group in enumerate(groups):
            keys, values = columns(group, head, False), columns(group, head, True)
            scores = lax.dot_general(q, keys, contract_last, preferred_element_type=jnp.float32)
            if number == len(groups) - 1:
                text_at = keys.shape[0] - arrays[group[-1][0]].shape[0]
                usable = lax.broadcasted_iota(jnp.int32, scores.shape, 1) < scalars[1] + text_at
                scores = jnp.where(usable, scores, -jnp.inf)
            block_top = jnp.max(scores, axis=1, keepdims=True)
            new_top = block_top if top is None else jnp.maximum(top, block_top)
            weights = jnp.exp2((scores - new_top) * EXP_SCALE)
            block_total = jnp.sum(weights, axis=1, keepdims=True)
            block_weighted = jnp.dot(weights.astype(jnp.bfloat16), values, preferred_element_type=jnp.float32)
            if top is None:
                total, weighted = block_total, block_weighted
            else:
                rescale = jnp.exp2((top - new_top) * EXP_SCALE)
                total, weighted = total * rescale + block_total, weighted * rescale + block_weighted
            top = new_top
        context = (weighted / total).astype(jnp.bfloat16)
        for index, out in enumerate(outs):
            out[:, here] = context[index * rows : (index + 1) * rows]


def attend_pair(scalars, queries, q_block, groups, earlier):
    n_q = len(queries)
    arrays, numbered = [], []
    for group in groups:
        numbered.append([])
        for array, key_column, value_column in group:
            numbered[-1].append((len(arrays), key_column, value_column))
            arrays.append(array)
    vmem = pl.BlockSpec(memory_space=pltpu.VMEM)
    return pl.pallas_call(
        functools.partial(attend_kernel, n_q, q_block * HEAD_DIM, numbered),
        in_specs=[pl.BlockSpec(memory_space=pltpu.SMEM)]
        + [vmem] * (n_q + len(arrays))
        + [pl.BlockSpec(memory_space=pl.ANY)] * len(earlier),
        out_specs=[vmem] * n_q,
        out_shape=[jax.ShapeDtypeStruct((queries[0].shape[0], PAIR), jnp.bfloat16)] * n_q,
        compiler_params=pltpu.CompilerParams(vmem_limit_bytes=24 * 2**20),
        cost_estimate=BIG,
        name="attend",
    )(scalars, *queries, *arrays, *earlier)


def text_kernel(planes, where, keys, values, *refs):
    out = refs[-1]
    slab = planes * PAIR
    for phase in range(keys.shape[1] // slab):
        columns = pl.ds(pl.multiple_of(phase * slab + where[0] * PAIR, PAIR), PAIR)
        out[:, 2 * phase * PAIR : (2 * phase + 1) * PAIR] = keys[:, columns]
        out[:, (2 * phase + 1) * PAIR : (2 * phase + 2) * PAIR] = values[:, columns]


def own_text(where, planes, text_keys, text_values, earlier):
    vmem = pl.BlockSpec(memory_space=pltpu.VMEM)
    shape = jax.ShapeDtypeStruct((text_keys.shape[0], 2 * text_keys.shape[1] // planes), text_keys.dtype)
    return pl.pallas_call(
        functools.partial(text_kernel, planes),
        in_specs=[pl.BlockSpec(memory_space=pltpu.SMEM), vmem, vmem]
        + [pl.BlockSpec(memory_space=pl.ANY)] * len(earlier),
        out_specs=vmem,
        out_shape=shape,
        compiler_params=pltpu.CompilerParams(vmem_limit_bytes=6 * 2**20),
        cost_estimate=SMALL,
        name="own_text",
    )(where, text_keys, text_values, *earlier)


def deltas_kernel(plan, deltas, *refs):
    out = refs[-1]
    total = plan[0].astype(jnp.float32) * deltas[0].astype(jnp.float32)
    for block in range(1, deltas.shape[0]):
        total = total + plan[block].astype(jnp.float32) * deltas[block].astype(jnp.float32)
    out[...] = total * 0.25


def sum_deltas(plan, deltas, earlier):
    blocks, rows, width = deltas.shape
    step = width // 4
    return pl.pallas_call(
        deltas_kernel,
        grid=(4,),
        in_specs=[
            pl.BlockSpec(memory_space=pltpu.SMEM),
            pl.BlockSpec((blocks, rows, step), lambda i: (0, 0, i)),
        ]
        + [pl.BlockSpec(memory_space=pl.ANY)] * len(earlier),
        out_specs=pl.BlockSpec((rows, step), lambda i: (0, i)),
        out_shape=jax.ShapeDtypeStruct((rows, width), jnp.float32),
        cost_estimate=SMALL,
        compiler_params=pltpu.CompilerParams(vmem_limit_bytes=6 * 2**20),
        name="deltas",
    )(plan, deltas, *earlier)


def mix_kernel(planes, where, added, *refs):
    pieces, out = refs[:-1], refs[-1]
    slab = planes * PAIR
    phase = 0
    for first in range(0, len(pieces), planes):
        for part in range(pieces[first].shape[1] // PAIR):
            for relative in range(planes):
                plane = jnp.bitwise_xor(where[0], relative)
                columns = pl.ds(pl.multiple_of(phase * slab + plane * PAIR, PAIR), PAIR)
                piece = pieces[first + relative][:, part * PAIR : (part + 1) * PAIR]
                out[:, columns] = (piece.astype(jnp.float32) + added[:, columns]).astype(out.dtype)
            phase += 1


def mix(where, planes, added, pieces):
    vmem = pl.BlockSpec(memory_space=pltpu.VMEM)
    return pl.pallas_call(
        functools.partial(mix_kernel, planes),
        in_specs=[pl.BlockSpec(memory_space=pltpu.SMEM)] + [vmem] * (1 + len(pieces)),
        out_specs=vmem,
        out_shape=jax.ShapeDtypeStruct(added.shape, jnp.bfloat16),
        compiler_params=pltpu.CompilerParams(vmem_limit_bytes=6 * 2**20),
        cost_estimate=SMALL,
        name="mix",
    )(where, added, *pieces)


def plane_body(queries, keys, values, text_keys, text_values, text_len, plan, deltas):
    size = lax.axis_size("seq")
    planes = size // PLANE
    slab = planes * PAIR
    plane = lax.axis_index("seq") // PLANE
    where = plane.astype(jnp.int32).reshape(1)
    scalars = jnp.concatenate([where, text_len])

    def swap(array, distance):
        return lax.ppermute(array, "seq", [(i, i ^ distance) for i in range(size)])

    def send(piece, r):
        return swap(piece, PLANE * r)

    def release(batch, lanes):
        return [(0, [batch[r]], None) for r in lanes]

    def sent(lanes, pieces):
        return {r: send(piece, r) for r, piece in zip(lanes, pieces)}

    def whole(batch, arrived):
        return [batch[0]] + [arrived[r] for r in range(1, planes)]

    def received_kv(arrived):
        return (0, [arrived[r] for r in range(1, planes)], 2 * PAIR)

    every = tuple(range(1, planes))
    fast, slow = every[-1:], every[:-1]
    *z1, own_all = first_pack(where, planes, keys, values)
    groups = [((1, 1), (2, 1)), ((1, 2), (2, 2), (0, 0)), ((0, 1), (0, 2))]
    z2, z3, z4 = pack(where, groups, planes, (queries, keys, values), z1)
    text = own_text(where, planes, text_keys, text_values, [z2[0]])
    added = sum_deltas(plan, deltas, [text])

    in1 = {r: send(z1[r], r) for r in every}
    own_other = swap(own_all, 2)
    out = tick(release(z2, fast), [added] + [in1[r] for r in fast], BIG)
    in2 = sent(fast, out)
    received1, *out = tick([received_kv(in1)] + release(z2, slow), [out[0]], MID)
    in2.update(sent(slow, out))
    other1 = swap(received1, 2)
    (own_pair,) = tick([(0, [own_all, own_other], None)], [received1], SMALL)
    own_core = swap(own_pair, 1)
    out = tick(release(z3, fast), [received1] + [in2[r] for r in fast], BIG)
    in3 = sent(fast, out)
    received2, *out = tick([received_kv(in2)] + release(z3, slow), [out[0]], MID)
    in3.update(sent(slow, out))
    (pair1,) = tick([(0, [other1, received1], None)], [received2], MID)
    other2, core1 = swap(received2, 2), swap(pair1, 1)
    out = tick(release(z4, fast), [received2] + [in3[r] for r in fast], BIG)
    in4 = sent(fast, out)
    received3, *out = tick([received_kv(in3)] + release(z4, slow), [out[0], core1, own_core], MID)
    in4.update(sent(slow, out))
    (pair2,) = tick([(0, [other2, received2], None)], [received3], MID)
    other3, core2 = swap(received3, 2), swap(pair2, 1)

    def heads(phase, pieces, block, pair, core, earlier):
        at = 2 * PAIR * phase
        mine = [(array, at, at + PAIR) for array in (own_all, own_other, own_core, text)]
        return attend_pair(scalars, pieces, block, [[(pair, 0, PAIR)], [(core, 0, PAIR)], mine], earlier)

    context1 = heads(0, whole(z3, in3), 4, pair1, core1, [received3, pair2] + [in4[r] for r in fast])
    context2 = heads(1, whole(z4, in4), 0, pair2, core2, [context1[0]])
    pair3, *contexts = tick(
        [(0, [other3, received3], None)] + [(1, [context1[r], context2[r]], None) for r in range(planes)], [], MID
    )
    core3 = swap(pair3, 1)
    returned = [contexts[0]] + [send(contexts[r], r) for r in every]
    context3 = heads(2, whole(z4, in4), 2, pair3, core3, [])
    returned += [context3[0]] + [send(context3[r], r) for r in every]
    return mix(where, planes, added, returned)


def attend(head_queries, head_keys, head_values, group_token_keys, group_tv, usable):
    query_rows = head_queries.shape[0]
    score_scale = HEAD_DIM ** (-0.5)
    reshaped_queries = head_queries.reshape(query_rows, HEADS_DEV, HEAD_DIM)

    def compute_scores(current_key_block):
        return (
            jnp.einsum(
                "qgp,ugp->gqu",
                reshaped_queries,
                current_key_block,
                preferred_element_type=jnp.float32,
            )
            * score_scale
        )

    text_scores = compute_scores(group_token_keys.reshape(-1, HEADS_DEV, HEAD_DIM))
    text_scores = jnp.where(usable[None, None, :], text_scores, -jnp.inf)
    row_top = jnp.max(text_scores, axis=-1)
    text_exp = jnp.exp(text_scores - row_top[..., None])
    denominator = jnp.sum(text_exp, axis=-1)
    weighted = jnp.einsum(
        "vie,evs->vis",
        text_exp.astype(jnp.bfloat16),
        group_tv.reshape(-1, HEADS_DEV, HEAD_DIM),
        preferred_element_type=jnp.float32,
    )
    key_total = head_keys.shape[0]
    current_key_block = 2048
    block_keys = head_keys.reshape(key_total // current_key_block, current_key_block, HEADS_DEV, HEAD_DIM)
    block_values = head_values.reshape(key_total // current_key_block, current_key_block, HEADS_DEV, HEAD_DIM)

    def advance(carry, blocks):
        old_top, old_denominator, old_weighted = carry
        local_keys, values_here = blocks
        block_scores = compute_scores(local_keys)
        new_top = jnp.maximum(old_top, jnp.max(block_scores, axis=-1))
        running_rescale = jnp.exp(old_top - new_top)
        block_exp = jnp.exp(block_scores - new_top[..., None])
        new_denominator = old_denominator * running_rescale + jnp.sum(block_exp, axis=-1)
        new_weighted = old_weighted * running_rescale[..., None] + jnp.einsum(
            "vie,evs->vis",
            block_exp.astype(jnp.bfloat16),
            values_here,
            preferred_element_type=jnp.float32,
        )
        return ((new_top, new_denominator, new_weighted), None)

    (row_top, denominator, weighted), unused = lax.scan(
        advance, (row_top, denominator, weighted), (block_keys, block_values)
    )
    context = weighted / denominator[..., None]
    return context.transpose(1, 0, 2).reshape(query_rows, HEADS_DEV * HEAD_DIM).astype(jnp.bfloat16)


def general_body(queries, keys, values, text_keys, text_values, text_len, plan, deltas):
    tok_rows, feat_width = queries.shape
    axis_count = lax.axis_size("seq")
    head_groups = HEADS // HEADS_DEV
    query_pieces = axis_count // head_groups
    slot_width = HEADS_DEV * HEAD_DIM

    def replicate_slots(array):
        spread = jnp.broadcast_to(array[:, None, :], (tok_rows, query_pieces, feat_width))
        return spread.reshape(tok_rows, query_pieces * feat_width)

    head_queries = lax.all_to_all(
        queries.reshape(tok_rows // query_pieces, query_pieces * feat_width),
        "seq",
        split_axis=1,
        concat_axis=0,
        tiled=True,
    )
    head_keys = lax.all_to_all(replicate_slots(keys), "seq", split_axis=1, concat_axis=0, tiled=True)
    head_values = lax.all_to_all(replicate_slots(values), "seq", split_axis=1, concat_axis=0, tiled=True)
    group_index = lax.axis_index("seq") % head_groups
    group_token_keys = lax.dynamic_slice_in_dim(text_keys, group_index * slot_width, slot_width, 1)
    group_tv = lax.dynamic_slice_in_dim(text_values, group_index * slot_width, slot_width, 1)
    usable = jnp.arange(text_keys.shape[0]) < text_len[0]
    context = attend(head_queries, head_keys, head_values, group_token_keys, group_tv, usable)
    returned = lax.all_to_all(context, "seq", split_axis=0, concat_axis=1, tiled=True)
    context_rows = returned.reshape(tok_rows, feat_width)
    added = (
        jnp.einsum("b,btc->tc", plan.astype(jnp.bfloat16), deltas, preferred_element_type=jnp.float32) * 0.25
    )
    return (context_rows.astype(jnp.float32) + added).astype(jnp.bfloat16)


def solution(mesh):
    size = mesh.shape["seq"]
    planes = size // PLANE
    fits = planes * PLANE == size and planes * 6 == HEADS
    return jax.shard_map(
        plane_body if fits else general_body,
        mesh=mesh,
        in_specs=(
            P(("grp", "seq"), None),
            P(("grp", "seq"), None),
            P(("grp", "seq"), None),
            P("grp", None),
            P("grp", None),
            P("grp"),
            P("grp"),
            P(None, ("grp", "seq"), None),
        ),
        out_specs=P(("grp", "seq"), None),
        check_vma=False,
    )
```

```python
import functools
import math

import jax
import jax.numpy as jnp
from jax import lax
from jax.experimental import pallas as pl
from jax.experimental.pallas import tpu as pltpu
from jax.sharding import PartitionSpec as P

HEADS = 24
HEAD_DIM = 128
HEADS_DEV = 3
PLANE = 4
PAIR = 2 * HEAD_DIM
EXP_SCALE = HEAD_DIM ** (-0.5) * math.log2(math.e)


SMALL = pl.CostEstimate(flops=1, bytes_accessed=1, transcendentals=0)
MID = pl.CostEstimate(flops=10**9, bytes_accessed=1, transcendentals=0)
BIG = pl.CostEstimate(flops=2 * 10**10, bytes_accessed=1, transcendentals=0)


def first_pack_kernel(planes, where, keys, values, *refs):
    outs, own = refs[:planes], refs[planes]
    slab = planes * PAIR
    for slot, source in enumerate((keys, values)):
        here = slice(slot * PAIR, (slot + 1) * PAIR)
        for relative, out in enumerate(outs):
            plane = jnp.bitwise_xor(where[0], relative)
            out[:, here] = source[:, pl.ds(pl.multiple_of(plane * PAIR, PAIR), PAIR)]
        for phase in range(keys.shape[1] // slab):
            start = pl.multiple_of(phase * slab + where[0] * PAIR, PAIR)
            at = (2 * phase + slot) * PAIR
            own[:, at : at + PAIR] = source[:, pl.ds(start, PAIR)]


def first_pack(where, planes, keys, values):
    rows, width = keys.shape
    vmem = pl.BlockSpec(memory_space=pltpu.VMEM)
    shapes = [jax.ShapeDtypeStruct((rows, 2 * PAIR), keys.dtype)] * planes
    shapes.append(jax.ShapeDtypeStruct((rows, 2 * width // planes), keys.dtype))
    return pl.pallas_call(
        functools.partial(first_pack_kernel, planes),
        out_shape=shapes,
        in_specs=[pl.BlockSpec(memory_space=pltpu.SMEM), vmem, vmem],
        out_specs=[vmem] * len(shapes),
        compiler_params=pltpu.CompilerParams(vmem_limit_bytes=6 * 2**20),
        cost_estimate=SMALL,
        name="first_pack",
    )(where, keys, values)


def pack_kernel(groups, planes, n_out, where, *refs):
    sources, outs = refs[:3], refs[-n_out:]
    slab = planes * PAIR
    for relative in range(planes):
        plane = jnp.bitwise_xor(where[0], relative)
        for index, spans in enumerate(groups):
            out = outs[index * planes + relative]
            for slot, (source, phase) in enumerate(spans):
                columns = pl.ds(pl.multiple_of(phase * slab + plane * PAIR, PAIR), PAIR)
                out[:, slot * PAIR : (slot + 1) * PAIR] = sources[source][:, columns]


def pack(where, groups, planes, sources, earlier):
    rows = sources[0].shape[0]
    shapes = [
        jax.ShapeDtypeStruct((rows, len(spans) * PAIR), sources[0].dtype) for spans in groups for _ in range(planes)
    ]
    vmem = pl.BlockSpec(memory_space=pltpu.VMEM)
    outs = pl.pallas_call(
        functools.partial(pack_kernel, groups, planes, len(shapes)),
        out_shape=shapes,
        in_specs=[pl.BlockSpec(memory_space=pltpu.SMEM)]
        + [vmem] * len(sources)
        + [pl.BlockSpec(memory_space=pl.ANY)] * len(earlier),
        out_specs=[vmem] * len(shapes),
        compiler_params=pltpu.CompilerParams(vmem_limit_bytes=8 * 2**20),
        cost_estimate=SMALL,
        name="pack",
    )(where, *sources, *earlier)
    return [outs[i * planes : (i + 1) * planes] for i in range(len(groups))]


def tick_kernel(axes, counts, widths, n_earlier, *refs):
    sources, outs = list(refs[n_earlier : n_earlier + sum(counts)]), refs[n_earlier + sum(counts) :]
    for axis, count, width, out in zip(axes, counts, widths, outs):
        at = 0
        for _ in range(count):
            source = sources.pop(0)
            if axis == 0:
                out[at : at + source.shape[0]] = source[:, :width]
                at += source.shape[0]
            else:
                out[:, at : at + source.shape[1]] = source[...]
                at += source.shape[1]


def tick(jobs, earlier, cost):
    axes = [axis for axis, _, _ in jobs]
    counts = [len(arrays) for _, arrays, _ in jobs]
    widths = [width or arrays[0].shape[1] for _, arrays, width in jobs]
    shapes = []
    for axis, arrays, width in jobs:
        if axis == 0:
            shape = (sum(a.shape[0] for a in arrays), width or arrays[0].shape[1])
        else:
            shape = (arrays[0].shape[0], sum(a.shape[1] for a in arrays))
        shapes.append(jax.ShapeDtypeStruct(shape, jnp.bfloat16))
    vmem = pl.BlockSpec(memory_space=pltpu.VMEM)
    return pl.pallas_call(
        functools.partial(tick_kernel, axes, counts, widths, len(earlier)),
        in_specs=[pl.BlockSpec(memory_space=pl.ANY)] * len(earlier) + [vmem] * sum(counts),
        out_specs=[vmem] * len(shapes),
        out_shape=shapes,
        compiler_params=pltpu.CompilerParams(vmem_limit_bytes=6 * 2**20),
        cost_estimate=cost,
        name="tick",
    )(*earlier, *[a for _, arrays, _ in jobs for a in arrays])


def attend_kernel(n_q, q_column, groups, scalars, *refs):
    queries, outs = refs[:n_q], refs[len(refs) - n_q :]
    arrays = refs[n_q:]
    rows = outs[0].shape[0]
    contract_last = (((1,), (1,)), ((), ()))

    def columns(group, head, which):
        parts = []
        for index, key_column, value_column in group:
            start = (value_column if which else key_column) + head * HEAD_DIM
            parts.append(arrays[index][:, start : start + HEAD_DIM])
        return parts[0] if len(parts) == 1 else jnp.concatenate(parts, axis=0)

    for head in range(2):
        here = slice(head * HEAD_DIM, (head + 1) * HEAD_DIM)
        q_here = slice(q_column + head * HEAD_DIM, q_column + (head + 1) * HEAD_DIM)
        q = jnp.concatenate([piece[:, q_here] for piece in queries], axis=0)
        top = None
        for number, group in enumerate(groups):
            keys, values = columns(group, head, False), columns(group, head, True)
            scores = lax.dot_general(q, keys, contract_last, preferred_element_type=jnp.float32)
            if number == len(groups) - 1:
                text_at = keys.shape[0] - arrays[group[-1][0]].shape[0]
                usable = lax.broadcasted_iota(jnp.int32, scores.shape, 1) < scalars[1] + text_at
                scores = jnp.where(usable, scores, -jnp.inf)
            block_top = jnp.max(scores, axis=1, keepdims=True)
            new_top = block_top if top is None else jnp.maximum(top, block_top)
            weights = jnp.exp2((scores - new_top) * EXP_SCALE).astype(jnp.bfloat16)
            extended = jnp.concatenate([values, jnp.ones_like(values)], axis=1)
            block_sums = jnp.dot(weights, extended, preferred_element_type=jnp.float32)
            sums = block_sums if top is None else sums * jnp.exp2((top - new_top) * EXP_SCALE) + block_sums
            top = new_top
        context = (sums[:, :HEAD_DIM] / sums[:, HEAD_DIM:]).astype(jnp.bfloat16)
        for index, out in enumerate(outs):
            out[:, here] = context[index * rows : (index + 1) * rows]


def attend_pair(scalars, queries, q_block, groups, earlier):
    n_q = len(queries)
    arrays, numbered = [], []
    for group in groups:
        numbered.append([])
        for array, key_column, value_column in group:
            numbered[-1].append((len(arrays), key_column, value_column))
            arrays.append(array)
    vmem = pl.BlockSpec(memory_space=pltpu.VMEM)
    return pl.pallas_call(
        functools.partial(attend_kernel, n_q, q_block * HEAD_DIM, numbered),
        in_specs=[pl.BlockSpec(memory_space=pltpu.SMEM)]
        + [vmem] * (n_q + len(arrays))
        + [pl.BlockSpec(memory_space=pl.ANY)] * len(earlier),
        out_specs=[vmem] * n_q,
        out_shape=[jax.ShapeDtypeStruct((queries[0].shape[0], PAIR), jnp.bfloat16)] * n_q,
        compiler_params=pltpu.CompilerParams(vmem_limit_bytes=24 * 2**20),
        cost_estimate=BIG,
        name="attend",
    )(scalars, *queries, *arrays, *earlier)


def text_kernel(planes, where, keys, values, *refs):
    out = refs[-1]
    slab = planes * PAIR
    for phase in range(keys.shape[1] // slab):
        columns = pl.ds(pl.multiple_of(phase * slab + where[0] * PAIR, PAIR), PAIR)
        out[:, 2 * phase * PAIR : (2 * phase + 1) * PAIR] = keys[:, columns]
        out[:, (2 * phase + 1) * PAIR : (2 * phase + 2) * PAIR] = values[:, columns]


def own_text(where, planes, text_keys, text_values, earlier):
    vmem = pl.BlockSpec(memory_space=pltpu.VMEM)
    shape = jax.ShapeDtypeStruct((text_keys.shape[0], 2 * text_keys.shape[1] // planes), text_keys.dtype)
    return pl.pallas_call(
        functools.partial(text_kernel, planes),
        in_specs=[pl.BlockSpec(memory_space=pltpu.SMEM), vmem, vmem]
        + [pl.BlockSpec(memory_space=pl.ANY)] * len(earlier),
        out_specs=vmem,
        out_shape=shape,
        compiler_params=pltpu.CompilerParams(vmem_limit_bytes=6 * 2**20),
        cost_estimate=SMALL,
        name="own_text",
    )(where, text_keys, text_values, *earlier)


def deltas_kernel(plan, deltas, *refs):
    out = refs[-1]
    total = plan[0].astype(jnp.float32) * deltas[0].astype(jnp.float32)
    for block in range(1, deltas.shape[0]):
        total = total + plan[block].astype(jnp.float32) * deltas[block].astype(jnp.float32)
    out[...] = total * 0.25


def sum_deltas(plan, deltas, earlier):
    blocks, rows, width = deltas.shape
    step = width // 4
    return pl.pallas_call(
        deltas_kernel,
        grid=(4,),
        in_specs=[
            pl.BlockSpec(memory_space=pltpu.SMEM),
            pl.BlockSpec((blocks, rows, step), lambda i: (0, 0, i)),
        ]
        + [pl.BlockSpec(memory_space=pl.ANY)] * len(earlier),
        out_specs=pl.BlockSpec((rows, step), lambda i: (0, i)),
        out_shape=jax.ShapeDtypeStruct((rows, width), jnp.float32),
        cost_estimate=SMALL,
        compiler_params=pltpu.CompilerParams(vmem_limit_bytes=6 * 2**20),
        name="deltas",
    )(plan, deltas, *earlier)


def mix_kernel(planes, places, where, added, *refs):
    out = refs[-1]
    for index, relative, phases in places:
        plane = jnp.bitwise_xor(where[0], relative)
        for part, phase in enumerate(phases):
            columns = pl.ds(pl.multiple_of((phase * planes + plane) * PAIR, PAIR), PAIR)
            piece = refs[index][:, part * PAIR : (part + 1) * PAIR]
            out[:, columns] = (piece.astype(jnp.float32) + added[:, columns]).astype(out.dtype)


def mix(where, planes, added, returned):
    places = [(index, relative, phases) for index, (_, relative, phases) in enumerate(returned)]
    pieces = [array for array, _, _ in returned]
    vmem = pl.BlockSpec(memory_space=pltpu.VMEM)
    return pl.pallas_call(
        functools.partial(mix_kernel, planes, places),
        in_specs=[pl.BlockSpec(memory_space=pltpu.SMEM)] + [vmem] * (1 + len(pieces)),
        out_specs=vmem,
        out_shape=jax.ShapeDtypeStruct(added.shape, jnp.bfloat16),
        compiler_params=pltpu.CompilerParams(vmem_limit_bytes=6 * 2**20),
        cost_estimate=SMALL,
        name="mix",
    )(where, added, *pieces)


def plane_body(queries, keys, values, text_keys, text_values, text_len, plan, deltas):
    size = lax.axis_size("seq")
    planes = size // PLANE
    slab = planes * PAIR
    plane = lax.axis_index("seq") // PLANE
    where = plane.astype(jnp.int32).reshape(1)
    scalars = jnp.concatenate([where, text_len])

    def swap(array, distance):
        return lax.ppermute(array, "seq", [(i, i ^ distance) for i in range(size)])

    def send(piece, r):
        return swap(piece, PLANE * r)

    def release(batch, lanes):
        return [(0, [batch[r]], None) for r in lanes]

    def sent(lanes, pieces):
        return {r: send(piece, r) for r, piece in zip(lanes, pieces)}

    def whole(batch, arrived):
        return [batch[0]] + [arrived[r] for r in range(1, planes)]

    def received_kv(arrived):
        return (0, [arrived[r] for r in range(1, planes)], 2 * PAIR)

    every = tuple(range(1, planes))
    fast, slow = every[-1:], every[:-1]
    *z1, own_all = first_pack(where, planes, keys, values)
    groups = [((1, 1), (2, 1)), ((1, 2), (2, 2), (0, 0)), ((0, 1), (0, 2))]
    z2, z3, z4 = pack(where, groups, planes, (queries, keys, values), z1)
    text = own_text(where, planes, text_keys, text_values, [z2[0]])
    added = sum_deltas(plan, deltas, [text])

    in1 = {r: send(z1[r], r) for r in every}
    own_other = swap(own_all, 2)
    out = tick(release(z2, fast), [added] + [in1[r] for r in fast], BIG)
    in2 = sent(fast, out)
    received1, *out = tick([received_kv(in1)] + release(z2, slow), [out[0]], MID)
    in2.update(sent(slow, out))
    other1 = swap(received1, 2)
    (own_pair,) = tick([(0, [own_all, own_other], None)], [received1], SMALL)
    own_core = swap(own_pair, 1)
    out = tick(release(z3, fast), [received1] + [in2[r] for r in fast], BIG)
    in3 = sent(fast, out)
    received2, *out = tick([received_kv(in2)] + release(z3, slow), [out[0]], MID)
    in3.update(sent(slow, out))
    (pair1,) = tick([(0, [other1, received1], None)], [received2], MID)
    other2, core1 = swap(received2, 2), swap(pair1, 1)
    out = tick(release(z4, fast), [received2] + [in3[r] for r in fast], BIG)
    in4 = sent(fast, out)
    received3, *out = tick([received_kv(in3)] + release(z4, slow), [out[0], core1, own_core], MID)
    in4.update(sent(slow, out))
    (pair2,) = tick([(0, [other2, received2], None)], [received3], MID)
    other3, core2 = swap(received3, 2), swap(pair2, 1)

    def heads(phase, pieces, block, pair, core, earlier):
        at = 2 * PAIR * phase
        near = [(pair, 0, PAIR), (own_all, at, at + PAIR), (own_other, at, at + PAIR)]
        far = [(core, 0, PAIR), (own_core, at, at + PAIR)]
        return attend_pair(scalars, pieces, block, [near, far, [(text, at, at + PAIR)]], earlier)

    context1 = heads(0, whole(z3, in3), 4, pair1, core1, [received3, pair2] + [in4[r] for r in fast])
    early = (3,)
    returned = [(send(context1[r], r), r, (0,)) for r in early]
    context2 = heads(1, whole(z4, in4), 0, pair2, core2, [context1[0]])
    late = [r for r in range(planes) if r not in early]
    pair3, *contexts = tick(
        [(0, [other3, received3], None)]
        + [(1, [context1[r], context2[r]], None) for r in late]
        + [(0, [context2[r]], None) for r in early],
        [array for array, _, _ in returned],
        MID,
    )
    core3 = swap(pair3, 1)
    for r, both in zip(late, contexts):
        returned.append((send(both, r) if r else both, r, (0, 1)))
    for r, one in zip(early, contexts[len(late) :]):
        returned.append((send(one, r), r, (1,)))
    context3 = heads(2, whole(z4, in4), 2, pair3, core3, [])
    returned += [(send(context3[r], r) if r else context3[r], r, (2,)) for r in range(planes)]
    return mix(where, planes, added, returned)


def attend(head_queries, head_keys, head_values, group_token_keys, group_tv, usable):
    query_rows = head_queries.shape[0]
    score_scale = HEAD_DIM ** (-0.5)
    reshaped_queries = head_queries.reshape(query_rows, HEADS_DEV, HEAD_DIM)

    def compute_scores(current_key_block):
        return (
            jnp.einsum(
                "qgp,ugp->gqu",
                reshaped_queries,
                current_key_block,
                preferred_element_type=jnp.float32,
            )
            * score_scale
        )

    text_scores = compute_scores(group_token_keys.reshape(-1, HEADS_DEV, HEAD_DIM))
    text_scores = jnp.where(usable[None, None, :], text_scores, -jnp.inf)
    row_top = jnp.max(text_scores, axis=-1)
    text_exp = jnp.exp(text_scores - row_top[..., None])
    denominator = jnp.sum(text_exp, axis=-1)
    weighted = jnp.einsum(
        "vie,evs->vis",
        text_exp.astype(jnp.bfloat16),
        group_tv.reshape(-1, HEADS_DEV, HEAD_DIM),
        preferred_element_type=jnp.float32,
    )
    key_total = head_keys.shape[0]
    current_key_block = 2048
    block_keys = head_keys.reshape(key_total // current_key_block, current_key_block, HEADS_DEV, HEAD_DIM)
    block_values = head_values.reshape(key_total // current_key_block, current_key_block, HEADS_DEV, HEAD_DIM)

    def advance(carry, blocks):
        old_top, old_denominator, old_weighted = carry
        local_keys, values_here = blocks
        block_scores = compute_scores(local_keys)
        new_top = jnp.maximum(old_top, jnp.max(block_scores, axis=-1))
        running_rescale = jnp.exp(old_top - new_top)
        block_exp = jnp.exp(block_scores - new_top[..., None])
        new_denominator = old_denominator * running_rescale + jnp.sum(block_exp, axis=-1)
        new_weighted = old_weighted * running_rescale[..., None] + jnp.einsum(
            "vie,evs->vis",
            block_exp.astype(jnp.bfloat16),
            values_here,
            preferred_element_type=jnp.float32,
        )
        return ((new_top, new_denominator, new_weighted), None)

    (row_top, denominator, weighted), unused = lax.scan(
        advance, (row_top, denominator, weighted), (block_keys, block_values)
    )
    context = weighted / denominator[..., None]
    return context.transpose(1, 0, 2).reshape(query_rows, HEADS_DEV * HEAD_DIM).astype(jnp.bfloat16)


def general_body(queries, keys, values, text_keys, text_values, text_len, plan, deltas):
    tok_rows, feat_width = queries.shape
    axis_count = lax.axis_size("seq")
    head_groups = HEADS // HEADS_DEV
    query_pieces = axis_count // head_groups
    slot_width = HEADS_DEV * HEAD_DIM

    def replicate_slots(array):
        spread = jnp.broadcast_to(array[:, None, :], (tok_rows, query_pieces, feat_width))
        return spread.reshape(tok_rows, query_pieces * feat_width)

    head_queries = lax.all_to_all(
        queries.reshape(tok_rows // query_pieces, query_pieces * feat_width),
        "seq",
        split_axis=1,
        concat_axis=0,
        tiled=True,
    )
    head_keys = lax.all_to_all(replicate_slots(keys), "seq", split_axis=1, concat_axis=0, tiled=True)
    head_values = lax.all_to_all(replicate_slots(values), "seq", split_axis=1, concat_axis=0, tiled=True)
    group_index = lax.axis_index("seq") % head_groups
    group_token_keys = lax.dynamic_slice_in_dim(text_keys, group_index * slot_width, slot_width, 1)
    group_tv = lax.dynamic_slice_in_dim(text_values, group_index * slot_width, slot_width, 1)
    usable = jnp.arange(text_keys.shape[0]) < text_len[0]
    context = attend(head_queries, head_keys, head_values, group_token_keys, group_tv, usable)
    returned = lax.all_to_all(context, "seq", split_axis=0, concat_axis=1, tiled=True)
    context_rows = returned.reshape(tok_rows, feat_width)
    added = (
        jnp.einsum("b,btc->tc", plan.astype(jnp.bfloat16), deltas, preferred_element_type=jnp.float32) * 0.25
    )
    return (context_rows.astype(jnp.float32) + added).astype(jnp.bfloat16)


def solution(mesh):
    size = mesh.shape["seq"]
    planes = size // PLANE
    fits = planes * PLANE == size and planes * 6 == HEADS
    return jax.shard_map(
        plane_body if fits else general_body,
        mesh=mesh,
        in_specs=(
            P(("grp", "seq"), None),
            P(("grp", "seq"), None),
            P(("grp", "seq"), None),
            P("grp", None),
            P("grp", None),
            P("grp"),
            P("grp"),
            P(None, ("grp", "seq"), None),
        ),
        out_specs=P(("grp", "seq"), None),
        check_vma=False,
    )
```

```python
import functools
import math

import jax
import jax.numpy as jnp
from jax import lax
from jax.experimental import pallas as pl
from jax.experimental.pallas import tpu as pltpu
from jax.sharding import PartitionSpec as P

HEADS = 24
HEAD_DIM = 128
HEADS_DEV = 3
PLANE = 4
PAIR = 2 * HEAD_DIM
EXP_SCALE = HEAD_DIM ** (-0.5) * math.log2(math.e)


SMALL = pl.CostEstimate(flops=1, bytes_accessed=1, transcendentals=0)
MID = pl.CostEstimate(flops=6 * 10**8, bytes_accessed=1, transcendentals=0)
BIG = pl.CostEstimate(flops=2 * 10**10, bytes_accessed=1, transcendentals=0)


def first_pack_kernel(planes, where, keys, values, *refs):
    outs, own = refs[:planes], refs[planes]
    slab = planes * PAIR
    for slot, source in enumerate((keys, values)):
        here = slice(slot * PAIR, (slot + 1) * PAIR)
        for relative, out in enumerate(outs):
            plane = jnp.bitwise_xor(where[0], relative)
            out[:, here] = source[:, pl.ds(pl.multiple_of(plane * PAIR, PAIR), PAIR)]
        for phase in range(keys.shape[1] // slab):
            start = pl.multiple_of(phase * slab + where[0] * PAIR, PAIR)
            at = (2 * phase + slot) * PAIR
            own[:, at : at + PAIR] = source[:, pl.ds(start, PAIR)]


def first_pack(where, planes, keys, values):
    rows, width = keys.shape
    vmem = pl.BlockSpec(memory_space=pltpu.VMEM)
    shapes = [jax.ShapeDtypeStruct((rows, 2 * PAIR), keys.dtype)] * planes
    shapes.append(jax.ShapeDtypeStruct((rows, 2 * width // planes), keys.dtype))
    return pl.pallas_call(
        functools.partial(first_pack_kernel, planes),
        out_shape=shapes,
        in_specs=[pl.BlockSpec(memory_space=pltpu.SMEM), vmem, vmem],
        out_specs=[vmem] * len(shapes),
        compiler_params=pltpu.CompilerParams(vmem_limit_bytes=6 * 2**20),
        cost_estimate=SMALL,
        name="first_pack",
    )(where, keys, values)


def pack_kernel(groups, planes, n_out, where, *refs):
    sources, outs = refs[:3], refs[-n_out:]
    slab = planes * PAIR
    for relative in range(planes):
        plane = jnp.bitwise_xor(where[0], relative)
        for index, spans in enumerate(groups):
            out = outs[index * planes + relative]
            for slot, (source, phase) in enumerate(spans):
                columns = pl.ds(pl.multiple_of(phase * slab + plane * PAIR, PAIR), PAIR)
                out[:, slot * PAIR : (slot + 1) * PAIR] = sources[source][:, columns]


def pack(where, groups, planes, sources, earlier):
    rows = sources[0].shape[0]
    shapes = [
        jax.ShapeDtypeStruct((rows, len(spans) * PAIR), sources[0].dtype) for spans in groups for _ in range(planes)
    ]
    vmem = pl.BlockSpec(memory_space=pltpu.VMEM)
    outs = pl.pallas_call(
        functools.partial(pack_kernel, groups, planes, len(shapes)),
        out_shape=shapes,
        in_specs=[pl.BlockSpec(memory_space=pltpu.SMEM)]
        + [vmem] * len(sources)
        + [pl.BlockSpec(memory_space=pl.ANY)] * len(earlier),
        out_specs=[vmem] * len(shapes),
        compiler_params=pltpu.CompilerParams(vmem_limit_bytes=8 * 2**20),
        cost_estimate=SMALL,
        name="pack",
    )(where, *sources, *earlier)
    return [outs[i * planes : (i + 1) * planes] for i in range(len(groups))]


def tick_kernel(axes, counts, widths, n_earlier, *refs):
    sources, outs = list(refs[n_earlier : n_earlier + sum(counts)]), refs[n_earlier + sum(counts) :]
    for axis, count, width, out in zip(axes, counts, widths, outs):
        at = 0
        for _ in range(count):
            source = sources.pop(0)
            if axis == 0:
                out[at : at + source.shape[0]] = source[:, :width]
                at += source.shape[0]
            else:
                out[:, at : at + source.shape[1]] = source[...]
                at += source.shape[1]


def tick(jobs, earlier, cost):
    axes = [axis for axis, _, _ in jobs]
    counts = [len(arrays) for _, arrays, _ in jobs]
    widths = [width or arrays[0].shape[1] for _, arrays, width in jobs]
    shapes = []
    for axis, arrays, width in jobs:
        if axis == 0:
            shape = (sum(a.shape[0] for a in arrays), width or arrays[0].shape[1])
        else:
            shape = (arrays[0].shape[0], sum(a.shape[1] for a in arrays))
        shapes.append(jax.ShapeDtypeStruct(shape, jnp.bfloat16))
    vmem = pl.BlockSpec(memory_space=pltpu.VMEM)
    return pl.pallas_call(
        functools.partial(tick_kernel, axes, counts, widths, len(earlier)),
        in_specs=[pl.BlockSpec(memory_space=pl.ANY)] * len(earlier) + [vmem] * sum(counts),
        out_specs=[vmem] * len(shapes),
        out_shape=shapes,
        compiler_params=pltpu.CompilerParams(vmem_limit_bytes=6 * 2**20),
        cost_estimate=cost,
        name="tick",
    )(*earlier, *[a for _, arrays, _ in jobs for a in arrays])


def attend_kernel(n_q, q_column, groups, scalars, *refs):
    queries, outs = refs[:n_q], refs[len(refs) - n_q :]
    arrays = refs[n_q:]
    rows = outs[0].shape[0]
    contract_last = (((1,), (1,)), ((), ()))

    def columns(group, head, which):
        parts = []
        for index, key_column, value_column in group:
            start = (value_column if which else key_column) + head * HEAD_DIM
            parts.append(arrays[index][:, start : start + HEAD_DIM])
        return parts[0] if len(parts) == 1 else jnp.concatenate(parts, axis=0)

    for head in range(2):
        here = slice(head * HEAD_DIM, (head + 1) * HEAD_DIM)
        q_here = slice(q_column + head * HEAD_DIM, q_column + (head + 1) * HEAD_DIM)
        q = jnp.concatenate([piece[:, q_here] for piece in queries], axis=0)
        top = None
        for number, group in enumerate(groups):
            keys, values = columns(group, head, False), columns(group, head, True)
            scores = lax.dot_general(q, keys, contract_last, preferred_element_type=jnp.float32)
            if number == len(groups) - 1:
                text_at = keys.shape[0] - arrays[group[-1][0]].shape[0]
                usable = lax.broadcasted_iota(jnp.int32, scores.shape, 1) < scalars[1] + text_at
                scores = jnp.where(usable, scores, -jnp.inf)
            block_top = jnp.max(scores, axis=1, keepdims=True)
            new_top = block_top if top is None else jnp.maximum(top, block_top)
            weights = jnp.exp2((scores - new_top) * EXP_SCALE).astype(jnp.bfloat16)
            extended = jnp.concatenate([values, jnp.ones_like(values)], axis=1)
            block_sums = jnp.dot(weights, extended, preferred_element_type=jnp.float32)
            sums = block_sums if top is None else sums * jnp.exp2((top - new_top) * EXP_SCALE) + block_sums
            top = new_top
        context = (sums[:, :HEAD_DIM] / sums[:, HEAD_DIM:]).astype(jnp.bfloat16)
        for index, out in enumerate(outs):
            out[:, here] = context[index * rows : (index + 1) * rows]


def attend_pair(scalars, queries, q_block, groups, earlier):
    n_q = len(queries)
    arrays, numbered = [], []
    for group in groups:
        numbered.append([])
        for array, key_column, value_column in group:
            numbered[-1].append((len(arrays), key_column, value_column))
            arrays.append(array)
    vmem = pl.BlockSpec(memory_space=pltpu.VMEM)
    return pl.pallas_call(
        functools.partial(attend_kernel, n_q, q_block * HEAD_DIM, numbered),
        in_specs=[pl.BlockSpec(memory_space=pltpu.SMEM)]
        + [vmem] * (n_q + len(arrays))
        + [pl.BlockSpec(memory_space=pl.ANY)] * len(earlier),
        out_specs=[vmem] * n_q,
        out_shape=[jax.ShapeDtypeStruct((queries[0].shape[0], PAIR), jnp.bfloat16)] * n_q,
        compiler_params=pltpu.CompilerParams(vmem_limit_bytes=24 * 2**20),
        cost_estimate=BIG,
        name="attend",
    )(scalars, *queries, *arrays, *earlier)


def text_kernel(planes, where, keys, values, *refs):
    out = refs[-1]
    slab = planes * PAIR
    for phase in range(keys.shape[1] // slab):
        columns = pl.ds(pl.multiple_of(phase * slab + where[0] * PAIR, PAIR), PAIR)
        out[:, 2 * phase * PAIR : (2 * phase + 1) * PAIR] = keys[:, columns]
        out[:, (2 * phase + 1) * PAIR : (2 * phase + 2) * PAIR] = values[:, columns]


def own_text(where, planes, text_keys, text_values, earlier):
    vmem = pl.BlockSpec(memory_space=pltpu.VMEM)
    shape = jax.ShapeDtypeStruct((text_keys.shape[0], 2 * text_keys.shape[1] // planes), text_keys.dtype)
    return pl.pallas_call(
        functools.partial(text_kernel, planes),
        in_specs=[pl.BlockSpec(memory_space=pltpu.SMEM), vmem, vmem]
        + [pl.BlockSpec(memory_space=pl.ANY)] * len(earlier),
        out_specs=vmem,
        out_shape=shape,
        compiler_params=pltpu.CompilerParams(vmem_limit_bytes=6 * 2**20),
        cost_estimate=SMALL,
        name="own_text",
    )(where, text_keys, text_values, *earlier)


def deltas_kernel(plan, deltas, *refs):
    out = refs[-1]
    total = plan[0].astype(jnp.float32) * deltas[0].astype(jnp.float32)
    for block in range(1, deltas.shape[0]):
        total = total + plan[block].astype(jnp.float32) * deltas[block].astype(jnp.float32)
    out[...] = total * 0.25


def sum_deltas(plan, deltas, earlier):
    blocks, rows, width = deltas.shape
    step = width // 4
    return pl.pallas_call(
        deltas_kernel,
        grid=(4,),
        in_specs=[
            pl.BlockSpec(memory_space=pltpu.SMEM),
            pl.BlockSpec((blocks, rows, step), lambda i: (0, 0, i)),
        ]
        + [pl.BlockSpec(memory_space=pl.ANY)] * len(earlier),
        out_specs=pl.BlockSpec((rows, step), lambda i: (0, i)),
        out_shape=jax.ShapeDtypeStruct((rows, width), jnp.float32),
        cost_estimate=SMALL,
        compiler_params=pltpu.CompilerParams(vmem_limit_bytes=6 * 2**20),
        name="deltas",
    )(plan, deltas, *earlier)


def mix_kernel(planes, places, where, added, *refs):
    out = refs[-1]
    for index, relative, phases in places:
        plane = jnp.bitwise_xor(where[0], relative)
        for part, phase in enumerate(phases):
            columns = pl.ds(pl.multiple_of((phase * planes + plane) * PAIR, PAIR), PAIR)
            piece = refs[index][:, part * PAIR : (part + 1) * PAIR]
            out[:, columns] = (piece.astype(jnp.float32) + added[:, columns]).astype(out.dtype)


def mix(where, planes, added, returned):
    places = [(index, relative, phases) for index, (_, relative, phases) in enumerate(returned)]
    pieces = [array for array, _, _ in returned]
    vmem = pl.BlockSpec(memory_space=pltpu.VMEM)
    return pl.pallas_call(
        functools.partial(mix_kernel, planes, places),
        in_specs=[pl.BlockSpec(memory_space=pltpu.SMEM)] + [vmem] * (1 + len(pieces)),
        out_specs=vmem,
        out_shape=jax.ShapeDtypeStruct(added.shape, jnp.bfloat16),
        compiler_params=pltpu.CompilerParams(vmem_limit_bytes=6 * 2**20),
        cost_estimate=SMALL,
        name="mix",
    )(where, added, *pieces)


def plane_body(queries, keys, values, text_keys, text_values, text_len, plan, deltas):
    size = lax.axis_size("seq")
    planes = size // PLANE
    slab = planes * PAIR
    plane = lax.axis_index("seq") // PLANE
    where = plane.astype(jnp.int32).reshape(1)
    scalars = jnp.concatenate([where, text_len])

    def swap(array, distance):
        return lax.ppermute(array, "seq", [(i, i ^ distance) for i in range(size)])

    def send(piece, r):
        return swap(piece, PLANE * r)

    def release(batch, lanes):
        return [(0, [batch[r]], None) for r in lanes]

    def sent(lanes, pieces):
        return {r: send(piece, r) for r, piece in zip(lanes, pieces)}

    def whole(batch, arrived):
        return [batch[0]] + [arrived[r] for r in range(1, planes)]

    def received_kv(arrived):
        return (0, [arrived[r] for r in range(1, planes)], 2 * PAIR)

    every = tuple(range(1, planes))
    fast, slow = every[-1:], every[:-1]
    *z1, own_all = first_pack(where, planes, keys, values)
    groups = [((1, 1), (2, 1)), ((1, 2), (2, 2), (0, 0)), ((0, 1), (0, 2))]
    z2, z3, z4 = pack(where, groups, planes, (queries, keys, values), z1)
    text = own_text(where, planes, text_keys, text_values, [z2[0]])
    added = sum_deltas(plan, deltas, [text])

    in1 = {r: send(z1[r], r) for r in every}
    own_other = swap(own_all, 2)
    out = tick(release(z2, fast), [added] + [in1[r] for r in fast], BIG)
    in2 = sent(fast, out)
    received1, *out = tick([received_kv(in1)] + release(z2, slow), [out[0]], MID)
    in2.update(sent(slow, out))
    other1 = swap(received1, 2)
    (own_pair,) = tick([(0, [own_all, own_other], None)], [received1], SMALL)
    own_core = swap(own_pair, 1)
    out = tick(release(z3, fast), [received1] + [in2[r] for r in fast], BIG)
    in3 = sent(fast, out)
    received2, *out = tick([received_kv(in2)] + release(z3, slow), [out[0], own_core], MID)
    in3.update(sent(slow, out))
    (pair1,) = tick([(0, [other1, received1], None)], [received2], MID)
    other2, core1 = swap(received2, 2), swap(pair1, 1)
    out = tick(release(z4, fast), [received2] + [in3[r] for r in fast], BIG)
    in4 = sent(fast, out)
    received3, *out = tick([received_kv(in3)] + release(z4, slow), [out[0], core1, own_core], MID)
    in4.update(sent(slow, out))
    (pair2,) = tick([(0, [other2, received2], None)], [received3], MID)
    other3, core2 = swap(received3, 2), swap(pair2, 1)

    def heads(phase, pieces, block, pair, core, earlier):
        at = 2 * PAIR * phase
        near = [(pair, 0, PAIR), (own_all, at, at + PAIR), (own_other, at, at + PAIR)]
        far = [(core, 0, PAIR), (own_core, at, at + PAIR)]
        return attend_pair(scalars, pieces, block, [near, far, [(text, at, at + PAIR)]], earlier)

    context1 = heads(0, whole(z3, in3), 4, pair1, core1, [received3, pair2] + [in4[r] for r in fast])
    early = (3,)
    returned = [(send(context1[r], r), r, (0,)) for r in early]
    context2 = heads(1, whole(z4, in4), 0, pair2, core2, [context1[0]])
    late = [r for r in range(planes) if r not in early]
    pair3, *contexts = tick(
        [(0, [other3, received3], None)]
        + [(1, [context1[r], context2[r]], None) for r in late]
        + [(0, [context2[r]], None) for r in early],
        [array for array, _, _ in returned],
        MID,
    )
    core3 = swap(pair3, 1)
    for r, both in zip(late, contexts):
        returned.append((send(both, r) if r else both, r, (0, 1)))
    for r, one in zip(early, contexts[len(late) :]):
        returned.append((send(one, r), r, (1,)))
    context3 = heads(2, whole(z4, in4), 2, pair3, core3, [])
    returned += [(send(context3[r], r) if r else context3[r], r, (2,)) for r in range(planes)]
    return mix(where, planes, added, returned)


def attend(head_queries, head_keys, head_values, group_token_keys, group_tv, usable):
    query_rows = head_queries.shape[0]
    score_scale = HEAD_DIM ** (-0.5)
    reshaped_queries = head_queries.reshape(query_rows, HEADS_DEV, HEAD_DIM)

    def compute_scores(current_key_block):
        return (
            jnp.einsum(
                "qgp,ugp->gqu",
                reshaped_queries,
                current_key_block,
                preferred_element_type=jnp.float32,
            )
            * score_scale
        )

    text_scores = compute_scores(group_token_keys.reshape(-1, HEADS_DEV, HEAD_DIM))
    text_scores = jnp.where(usable[None, None, :], text_scores, -jnp.inf)
    row_top = jnp.max(text_scores, axis=-1)
    text_exp = jnp.exp(text_scores - row_top[..., None])
    denominator = jnp.sum(text_exp, axis=-1)
    weighted = jnp.einsum(
        "vie,evs->vis",
        text_exp.astype(jnp.bfloat16),
        group_tv.reshape(-1, HEADS_DEV, HEAD_DIM),
        preferred_element_type=jnp.float32,
    )
    key_total = head_keys.shape[0]
    current_key_block = 2048
    block_keys = head_keys.reshape(key_total // current_key_block, current_key_block, HEADS_DEV, HEAD_DIM)
    block_values = head_values.reshape(key_total // current_key_block, current_key_block, HEADS_DEV, HEAD_DIM)

    def advance(carry, blocks):
        old_top, old_denominator, old_weighted = carry
        local_keys, values_here = blocks
        block_scores = compute_scores(local_keys)
        new_top = jnp.maximum(old_top, jnp.max(block_scores, axis=-1))
        running_rescale = jnp.exp(old_top - new_top)
        block_exp = jnp.exp(block_scores - new_top[..., None])
        new_denominator = old_denominator * running_rescale + jnp.sum(block_exp, axis=-1)
        new_weighted = old_weighted * running_rescale[..., None] + jnp.einsum(
            "vie,evs->vis",
            block_exp.astype(jnp.bfloat16),
            values_here,
            preferred_element_type=jnp.float32,
        )
        return ((new_top, new_denominator, new_weighted), None)

    (row_top, denominator, weighted), unused = lax.scan(
        advance, (row_top, denominator, weighted), (block_keys, block_values)
    )
    context = weighted / denominator[..., None]
    return context.transpose(1, 0, 2).reshape(query_rows, HEADS_DEV * HEAD_DIM).astype(jnp.bfloat16)


def general_body(queries, keys, values, text_keys, text_values, text_len, plan, deltas):
    tok_rows, feat_width = queries.shape
    axis_count = lax.axis_size("seq")
    head_groups = HEADS // HEADS_DEV
    query_pieces = axis_count // head_groups
    slot_width = HEADS_DEV * HEAD_DIM

    def replicate_slots(array):
        spread = jnp.broadcast_to(array[:, None, :], (tok_rows, query_pieces, feat_width))
        return spread.reshape(tok_rows, query_pieces * feat_width)

    head_queries = lax.all_to_all(
        queries.reshape(tok_rows // query_pieces, query_pieces * feat_width),
        "seq",
        split_axis=1,
        concat_axis=0,
        tiled=True,
    )
    head_keys = lax.all_to_all(replicate_slots(keys), "seq", split_axis=1, concat_axis=0, tiled=True)
    head_values = lax.all_to_all(replicate_slots(values), "seq", split_axis=1, concat_axis=0, tiled=True)
    group_index = lax.axis_index("seq") % head_groups
    group_token_keys = lax.dynamic_slice_in_dim(text_keys, group_index * slot_width, slot_width, 1)
    group_tv = lax.dynamic_slice_in_dim(text_values, group_index * slot_width, slot_width, 1)
    usable = jnp.arange(text_keys.shape[0]) < text_len[0]
    context = attend(head_queries, head_keys, head_values, group_token_keys, group_tv, usable)
    returned = lax.all_to_all(context, "seq", split_axis=0, concat_axis=1, tiled=True)
    context_rows = returned.reshape(tok_rows, feat_width)
    added = (
        jnp.einsum("b,btc->tc", plan.astype(jnp.bfloat16), deltas, preferred_element_type=jnp.float32) * 0.25
    )
    return (context_rows.astype(jnp.float32) + added).astype(jnp.bfloat16)


def solution(mesh):
    size = mesh.shape["seq"]
    planes = size // PLANE
    fits = planes * PLANE == size and planes * 6 == HEADS
    return jax.shard_map(
        plane_body if fits else general_body,
        mesh=mesh,
        in_specs=(
            P(("grp", "seq"), None),
            P(("grp", "seq"), None),
            P(("grp", "seq"), None),
            P("grp", None),
            P("grp", None),
            P("grp"),
            P("grp"),
            P(None, ("grp", "seq"), None),
        ),
        out_specs=P(("grp", "seq"), None),
        check_vma=False,
    )
```

```python
import functools
import math

import jax
import jax.numpy as jnp
from jax import lax
from jax.experimental import pallas as pl
from jax.experimental.pallas import tpu as pltpu
from jax.sharding import PartitionSpec as P

HEADS = 24
HEAD_DIM = 128
HEADS_DEV = 3
PLANE = 4
PAIR = 2 * HEAD_DIM
EXP_SCALE = HEAD_DIM ** (-0.5) * math.log2(math.e)


SMALL = pl.CostEstimate(flops=1, bytes_accessed=1, transcendentals=0)
MID = pl.CostEstimate(flops=6 * 10**8, bytes_accessed=1, transcendentals=0)
BIG = pl.CostEstimate(flops=2 * 10**10, bytes_accessed=1, transcendentals=0)


def first_pack_kernel(planes, where, keys, values, *refs):
    outs, own = refs[:planes], refs[planes]
    slab = planes * PAIR
    for slot, source in enumerate((keys, values)):
        here = slice(slot * PAIR, (slot + 1) * PAIR)
        for relative, out in enumerate(outs):
            plane = jnp.bitwise_xor(where[0], relative)
            out[:, here] = source[:, pl.ds(pl.multiple_of(plane * PAIR, PAIR), PAIR)]
        for phase in range(keys.shape[1] // slab):
            start = pl.multiple_of(phase * slab + where[0] * PAIR, PAIR)
            at = (2 * phase + slot) * PAIR
            own[:, at : at + PAIR] = source[:, pl.ds(start, PAIR)]


def first_pack(where, planes, keys, values):
    rows, width = keys.shape
    vmem = pl.BlockSpec(memory_space=pltpu.VMEM)
    shapes = [jax.ShapeDtypeStruct((rows, 2 * PAIR), keys.dtype)] * planes
    shapes.append(jax.ShapeDtypeStruct((rows, 2 * width // planes), keys.dtype))
    return pl.pallas_call(
        functools.partial(first_pack_kernel, planes),
        out_shape=shapes,
        in_specs=[pl.BlockSpec(memory_space=pltpu.SMEM), vmem, vmem],
        out_specs=[vmem] * len(shapes),
        compiler_params=pltpu.CompilerParams(vmem_limit_bytes=6 * 2**20),
        cost_estimate=SMALL,
        name="first_pack",
    )(where, keys, values)


def pack_kernel(groups, planes, n_out, where, *refs):
    sources, outs = refs[:3], refs[-n_out:]
    slab = planes * PAIR
    for relative in range(planes):
        plane = jnp.bitwise_xor(where[0], relative)
        for index, spans in enumerate(groups):
            out = outs[index * planes + relative]
            for slot, (source, phase) in enumerate(spans):
                columns = pl.ds(pl.multiple_of(phase * slab + plane * PAIR, PAIR), PAIR)
                out[:, slot * PAIR : (slot + 1) * PAIR] = sources[source][:, columns]


def pack(where, groups, planes, sources, earlier):
    rows = sources[0].shape[0]
    shapes = [
        jax.ShapeDtypeStruct((rows, len(spans) * PAIR), sources[0].dtype) for spans in groups for _ in range(planes)
    ]
    vmem = pl.BlockSpec(memory_space=pltpu.VMEM)
    outs = pl.pallas_call(
        functools.partial(pack_kernel, groups, planes, len(shapes)),
        out_shape=shapes,
        in_specs=[pl.BlockSpec(memory_space=pltpu.SMEM)]
        + [vmem] * len(sources)
        + [pl.BlockSpec(memory_space=pl.ANY)] * len(earlier),
        out_specs=[vmem] * len(shapes),
        compiler_params=pltpu.CompilerParams(vmem_limit_bytes=8 * 2**20),
        cost_estimate=SMALL,
        name="pack",
    )(where, *sources, *earlier)
    return [outs[i * planes : (i + 1) * planes] for i in range(len(groups))]


def tick_kernel(axes, counts, widths, n_earlier, *refs):
    sources, outs = list(refs[n_earlier : n_earlier + sum(counts)]), refs[n_earlier + sum(counts) :]
    for axis, count, width, out in zip(axes, counts, widths, outs):
        at = 0
        for _ in range(count):
            source = sources.pop(0)
            if axis == 0:
                out[at : at + source.shape[0]] = source[:, :width]
                at += source.shape[0]
            else:
                out[:, at : at + source.shape[1]] = source[...]
                at += source.shape[1]


def tick(jobs, earlier, cost):
    axes = [axis for axis, _, _ in jobs]
    counts = [len(arrays) for _, arrays, _ in jobs]
    widths = [width or arrays[0].shape[1] for _, arrays, width in jobs]
    shapes = []
    for axis, arrays, width in jobs:
        if axis == 0:
            shape = (sum(a.shape[0] for a in arrays), width or arrays[0].shape[1])
        else:
            shape = (arrays[0].shape[0], sum(a.shape[1] for a in arrays))
        shapes.append(jax.ShapeDtypeStruct(shape, jnp.bfloat16))
    vmem = pl.BlockSpec(memory_space=pltpu.VMEM)
    return pl.pallas_call(
        functools.partial(tick_kernel, axes, counts, widths, len(earlier)),
        in_specs=[pl.BlockSpec(memory_space=pl.ANY)] * len(earlier) + [vmem] * sum(counts),
        out_specs=[vmem] * len(shapes),
        out_shape=shapes,
        compiler_params=pltpu.CompilerParams(vmem_limit_bytes=6 * 2**20),
        cost_estimate=cost,
        name="tick",
    )(*earlier, *[a for _, arrays, _ in jobs for a in arrays])


def attend_kernel(n_q, q_column, groups, scalars, *refs):
    queries, outs = refs[:n_q], refs[len(refs) - n_q :]
    arrays = refs[n_q:]
    rows = outs[0].shape[0]
    contract_last = (((1,), (1,)), ((), ()))

    def columns(group, head, which):
        parts = []
        for index, key_column, value_column in group:
            start = (value_column if which else key_column) + head * HEAD_DIM
            parts.append(arrays[index][:, start : start + HEAD_DIM])
        return parts[0] if len(parts) == 1 else jnp.concatenate(parts, axis=0)

    for head in range(2):
        here = slice(head * HEAD_DIM, (head + 1) * HEAD_DIM)
        q_here = slice(q_column + head * HEAD_DIM, q_column + (head + 1) * HEAD_DIM)
        q = jnp.concatenate([piece[:, q_here] for piece in queries], axis=0)
        top = None
        for number, group in enumerate(groups):
            keys, values = columns(group, head, False), columns(group, head, True)
            scores = lax.dot_general(q, keys, contract_last, preferred_element_type=jnp.float32)
            if number == len(groups) - 1:
                text_at = keys.shape[0] - arrays[group[-1][0]].shape[0]
                usable = lax.broadcasted_iota(jnp.int32, scores.shape, 1) < scalars[1] + text_at
                scores = jnp.where(usable, scores, -jnp.inf)
            block_top = jnp.max(scores, axis=1, keepdims=True)
            new_top = block_top if top is None else jnp.maximum(top, block_top)
            weights = jnp.exp2((scores - new_top) * EXP_SCALE).astype(jnp.bfloat16)
            extended = jnp.concatenate([values, jnp.ones_like(values)], axis=1)
            block_sums = jnp.dot(weights, extended, preferred_element_type=jnp.float32)
            sums = block_sums if top is None else sums * jnp.exp2((top - new_top) * EXP_SCALE) + block_sums
            top = new_top
        context = (sums[:, :HEAD_DIM] / sums[:, HEAD_DIM:]).astype(jnp.bfloat16)
        for index, out in enumerate(outs):
            out[:, here] = context[index * rows : (index + 1) * rows]


def attend_pair(scalars, queries, q_block, groups, earlier):
    n_q = len(queries)
    arrays, numbered = [], []
    for group in groups:
        numbered.append([])
        for array, key_column, value_column in group:
            numbered[-1].append((len(arrays), key_column, value_column))
            arrays.append(array)
    vmem = pl.BlockSpec(memory_space=pltpu.VMEM)
    return pl.pallas_call(
        functools.partial(attend_kernel, n_q, q_block * HEAD_DIM, numbered),
        in_specs=[pl.BlockSpec(memory_space=pltpu.SMEM)]
        + [vmem] * (n_q + len(arrays))
        + [pl.BlockSpec(memory_space=pl.ANY)] * len(earlier),
        out_specs=[vmem] * n_q,
        out_shape=[jax.ShapeDtypeStruct((queries[0].shape[0], PAIR), jnp.bfloat16)] * n_q,
        compiler_params=pltpu.CompilerParams(vmem_limit_bytes=24 * 2**20),
        cost_estimate=BIG,
        name="attend",
    )(scalars, *queries, *arrays, *earlier)


def text_kernel(planes, where, keys, values, *refs):
    out = refs[-1]
    slab = planes * PAIR
    for phase in range(keys.shape[1] // slab):
        columns = pl.ds(pl.multiple_of(phase * slab + where[0] * PAIR, PAIR), PAIR)
        out[:, 2 * phase * PAIR : (2 * phase + 1) * PAIR] = keys[:, columns]
        out[:, (2 * phase + 1) * PAIR : (2 * phase + 2) * PAIR] = values[:, columns]


def own_text(where, planes, text_keys, text_values, earlier):
    vmem = pl.BlockSpec(memory_space=pltpu.VMEM)
    shape = jax.ShapeDtypeStruct((text_keys.shape[0], 2 * text_keys.shape[1] // planes), text_keys.dtype)
    return pl.pallas_call(
        functools.partial(text_kernel, planes),
        in_specs=[pl.BlockSpec(memory_space=pltpu.SMEM), vmem, vmem]
        + [pl.BlockSpec(memory_space=pl.ANY)] * len(earlier),
        out_specs=vmem,
        out_shape=shape,
        compiler_params=pltpu.CompilerParams(vmem_limit_bytes=6 * 2**20),
        cost_estimate=SMALL,
        name="own_text",
    )(where, text_keys, text_values, *earlier)


def deltas_kernel(plan, deltas, *refs):
    out = refs[-1]
    total = plan[0].astype(jnp.float32) * deltas[0].astype(jnp.float32)
    for block in range(1, deltas.shape[0]):
        total = total + plan[block].astype(jnp.float32) * deltas[block].astype(jnp.float32)
    out[...] = total * 0.25


def sum_deltas(plan, deltas, earlier):
    blocks, rows, width = deltas.shape
    step = width // 4
    return pl.pallas_call(
        deltas_kernel,
        grid=(4,),
        in_specs=[
            pl.BlockSpec(memory_space=pltpu.SMEM),
            pl.BlockSpec((blocks, rows, step), lambda i: (0, 0, i)),
        ]
        + [pl.BlockSpec(memory_space=pl.ANY)] * len(earlier),
        out_specs=pl.BlockSpec((rows, step), lambda i: (0, i)),
        out_shape=jax.ShapeDtypeStruct((rows, width), jnp.float32),
        cost_estimate=SMALL,
        compiler_params=pltpu.CompilerParams(vmem_limit_bytes=6 * 2**20),
        name="deltas",
    )(plan, deltas, *earlier)


def mix_kernel(planes, places, where, added, *refs):
    out = refs[-1]
    for index, relative, phases in places:
        plane = jnp.bitwise_xor(where[0], relative)
        for part, phase in enumerate(phases):
            columns = pl.ds(pl.multiple_of((phase * planes + plane) * PAIR, PAIR), PAIR)
            piece = refs[index][:, part * PAIR : (part + 1) * PAIR]
            out[:, columns] = (piece.astype(jnp.float32) + added[:, columns]).astype(out.dtype)


def mix(where, planes, added, returned):
    places = [(index, relative, phases) for index, (_, relative, phases) in enumerate(returned)]
    pieces = [array for array, _, _ in returned]
    vmem = pl.BlockSpec(memory_space=pltpu.VMEM)
    return pl.pallas_call(
        functools.partial(mix_kernel, planes, places),
        in_specs=[pl.BlockSpec(memory_space=pltpu.SMEM)] + [vmem] * (1 + len(pieces)),
        out_specs=vmem,
        out_shape=jax.ShapeDtypeStruct(added.shape, jnp.bfloat16),
        compiler_params=pltpu.CompilerParams(vmem_limit_bytes=6 * 2**20),
        cost_estimate=SMALL,
        name="mix",
    )(where, added, *pieces)


def plane_body(queries, keys, values, text_keys, text_values, text_len, plan, deltas):
    size = lax.axis_size("seq")
    planes = size // PLANE
    slab = planes * PAIR
    plane = lax.axis_index("seq") // PLANE
    where = plane.astype(jnp.int32).reshape(1)
    scalars = jnp.concatenate([where, text_len])

    def swap(array, distance):
        return lax.ppermute(array, "seq", [(i, i ^ distance) for i in range(size)])

    def send(piece, r):
        return swap(piece, PLANE * r)

    def release(batch, lanes):
        return [(0, [batch[r]], None) for r in lanes]

    def sent(lanes, pieces):
        return {r: send(piece, r) for r, piece in zip(lanes, pieces)}

    def whole(batch, arrived):
        return [batch[0]] + [arrived[r] for r in range(1, planes)]

    def received_kv(arrived):
        return (0, [arrived[r] for r in range(1, planes)], 2 * PAIR)

    every = tuple(range(1, planes))
    fast, slow = every[-1:], every[:-1]
    *z1, own_all = first_pack(where, planes, keys, values)
    groups = [((1, 1), (2, 1)), ((1, 2), (2, 2), (0, 0)), ((0, 1), (0, 2))]
    z2, z3, z4 = pack(where, groups, planes, (queries, keys, values), z1)
    text = own_text(where, planes, text_keys, text_values, [z2[0]])
    added = sum_deltas(plan, deltas, [text])

    in1 = {r: send(z1[r], r) for r in every}
    own_other = swap(own_all, 2)
    out = tick(release(z2, fast), [added] + [in1[r] for r in fast], BIG)
    in2 = sent(fast, out)
    received1, *out = tick([received_kv(in1)] + release(z2, slow), [out[0]], MID)
    in2.update(sent(slow, out))
    other1 = swap(received1, 2)
    (own_pair,) = tick([(0, [own_all, own_other], None)], [received1], SMALL)
    own_core = swap(own_pair, 1)
    out = tick(release(z3, fast), [received1] + [in2[r] for r in fast], BIG)
    in3 = sent(fast, out)
    received2, *out = tick([received_kv(in2)] + release(z3, slow), [out[0], own_core], MID)
    in3.update(sent(slow, out))
    (pair1,) = tick([(0, [other1, received1], None)], [received2], MID)
    other2, core1 = swap(received2, 2), swap(pair1, 1)
    out = tick(release(z4, fast), [received2] + [in3[r] for r in fast], BIG)
    in4 = sent(fast, out)
    received3, *out = tick([received_kv(in3)] + release(z4, slow), [out[0], core1, own_core], MID)
    in4.update(sent(slow, out))
    (pair2,) = tick([(0, [other2, received2], None)], [received3], MID)
    other3, core2 = swap(received3, 2), swap(pair2, 1)

    def heads(phase, pieces, block, pair, core, earlier):
        at = 2 * PAIR * phase
        near = [(pair, 0, PAIR), (own_all, at, at + PAIR), (own_other, at, at + PAIR)]
        far = [(core, 0, PAIR), (own_core, at, at + PAIR)]
        return attend_pair(scalars, pieces, block, [near, far, [(text, at, at + PAIR)]], earlier)

    context1 = heads(0, whole(z3, in3), 4, pair1, core1, [received3, pair2] + [in4[r] for r in fast])
    early = (2,)
    returned = [(send(context1[r], r), r, (0,)) for r in early]
    context2 = heads(1, whole(z4, in4), 0, pair2, core2, [context1[0]])
    late = [r for r in range(planes) if r not in early]
    pair3, *contexts = tick(
        [(0, [other3, received3], None)]
        + [(1, [context1[r], context2[r]], None) for r in late]
        + [(0, [context2[r]], None) for r in early],
        [],
        MID,
    )
    core3 = swap(pair3, 1)
    for r, both in zip(late, contexts):
        returned.append((send(both, r) if r else both, r, (0, 1)))
    for r, one in zip(early, contexts[len(late) :]):
        returned.append((send(one, r), r, (1,)))
    context3 = heads(2, whole(z4, in4), 2, pair3, core3, [])
    returned += [(send(context3[r], r) if r else context3[r], r, (2,)) for r in range(planes)]
    return mix(where, planes, added, returned)


def attend(head_queries, head_keys, head_values, group_token_keys, group_tv, usable):
    query_rows = head_queries.shape[0]
    score_scale = HEAD_DIM ** (-0.5)
    reshaped_queries = head_queries.reshape(query_rows, HEADS_DEV, HEAD_DIM)

    def compute_scores(current_key_block):
        return (
            jnp.einsum(
                "qgp,ugp->gqu",
                reshaped_queries,
                current_key_block,
                preferred_element_type=jnp.float32,
            )
            * score_scale
        )

    text_scores = compute_scores(group_token_keys.reshape(-1, HEADS_DEV, HEAD_DIM))
    text_scores = jnp.where(usable[None, None, :], text_scores, -jnp.inf)
    row_top = jnp.max(text_scores, axis=-1)
    text_exp = jnp.exp(text_scores - row_top[..., None])
    denominator = jnp.sum(text_exp, axis=-1)
    weighted = jnp.einsum(
        "vie,evs->vis",
        text_exp.astype(jnp.bfloat16),
        group_tv.reshape(-1, HEADS_DEV, HEAD_DIM),
        preferred_element_type=jnp.float32,
    )
    key_total = head_keys.shape[0]
    current_key_block = 2048
    block_keys = head_keys.reshape(key_total // current_key_block, current_key_block, HEADS_DEV, HEAD_DIM)
    block_values = head_values.reshape(key_total // current_key_block, current_key_block, HEADS_DEV, HEAD_DIM)

    def advance(carry, blocks):
        old_top, old_denominator, old_weighted = carry
        local_keys, values_here = blocks
        block_scores = compute_scores(local_keys)
        new_top = jnp.maximum(old_top, jnp.max(block_scores, axis=-1))
        running_rescale = jnp.exp(old_top - new_top)
        block_exp = jnp.exp(block_scores - new_top[..., None])
        new_denominator = old_denominator * running_rescale + jnp.sum(block_exp, axis=-1)
        new_weighted = old_weighted * running_rescale[..., None] + jnp.einsum(
            "vie,evs->vis",
            block_exp.astype(jnp.bfloat16),
            values_here,
            preferred_element_type=jnp.float32,
        )
        return ((new_top, new_denominator, new_weighted), None)

    (row_top, denominator, weighted), unused = lax.scan(
        advance, (row_top, denominator, weighted), (block_keys, block_values)
    )
    context = weighted / denominator[..., None]
    return context.transpose(1, 0, 2).reshape(query_rows, HEADS_DEV * HEAD_DIM).astype(jnp.bfloat16)


def general_body(queries, keys, values, text_keys, text_values, text_len, plan, deltas):
    tok_rows, feat_width = queries.shape
    axis_count = lax.axis_size("seq")
    head_groups = HEADS // HEADS_DEV
    query_pieces = axis_count // head_groups
    slot_width = HEADS_DEV * HEAD_DIM

    def replicate_slots(array):
        spread = jnp.broadcast_to(array[:, None, :], (tok_rows, query_pieces, feat_width))
        return spread.reshape(tok_rows, query_pieces * feat_width)

    head_queries = lax.all_to_all(
        queries.reshape(tok_rows // query_pieces, query_pieces * feat_width),
        "seq",
        split_axis=1,
        concat_axis=0,
        tiled=True,
    )
    head_keys = lax.all_to_all(replicate_slots(keys), "seq", split_axis=1, concat_axis=0, tiled=True)
    head_values = lax.all_to_all(replicate_slots(values), "seq", split_axis=1, concat_axis=0, tiled=True)
    group_index = lax.axis_index("seq") % head_groups
    group_token_keys = lax.dynamic_slice_in_dim(text_keys, group_index * slot_width, slot_width, 1)
    group_tv = lax.dynamic_slice_in_dim(text_values, group_index * slot_width, slot_width, 1)
    usable = jnp.arange(text_keys.shape[0]) < text_len[0]
    context = attend(head_queries, head_keys, head_values, group_token_keys, group_tv, usable)
    returned = lax.all_to_all(context, "seq", split_axis=0, concat_axis=1, tiled=True)
    context_rows = returned.reshape(tok_rows, feat_width)
    added = (
        jnp.einsum("b,btc->tc", plan.astype(jnp.bfloat16), deltas, preferred_element_type=jnp.float32) * 0.25
    )
    return (context_rows.astype(jnp.float32) + added).astype(jnp.bfloat16)


def solution(mesh):
    size = mesh.shape["seq"]
    planes = size // PLANE
    fits = planes * PLANE == size and planes * 6 == HEADS
    return jax.shard_map(
        plane_body if fits else general_body,
        mesh=mesh,
        in_specs=(
            P(("grp", "seq"), None),
            P(("grp", "seq"), None),
            P(("grp", "seq"), None),
            P("grp", None),
            P("grp", None),
            P("grp"),
            P("grp"),
            P(None, ("grp", "seq"), None),
        ),
        out_specs=P(("grp", "seq"), None),
        check_vma=False,
    )
```
